32 devices in a mesh: row: 4 (over y, x), col: 8 (over z, core).
Axes of the slice: x: 2, y: 2, z: 4, core: 2. Of those that a mesh axis runs over, the one named last changes fastest.
Arguments:
- images: float32 [64, 28, 28, 3], P(('row', 'col')), may hold values from -6 to 6
- noise_field: float32 [64, 28, 28, 3], P(('row', 'col')), may hold values from -6 to 6
- stem_weight: bfloat16 [27, 256], replicated, may hold values from -1.25 to 1.25
- level_one: bfloat16 [4, 2304, 256], replicated, may hold values from -0.125 to 0.125
- down_weight: bfloat16 [1024, 256], replicated, may hold values from -0.1875 to 0.1875
- level_two: bfloat16 [2, 2304, 256], replicated, may hold values from -0.125 to 0.125
- up_weight: bfloat16 [256, 1024], replicated, may hold values from -0.375 to 0.375
- out_weight: bfloat16 [256, 3], replicated, may hold values from -0.375 to 0.375
- embed_weight: bfloat16 [588, 6144], replicated
- embed_bias: float32 [6144], replicated
- mlp_in: bfloat16 [6144, 24576], P('col', 'row'), may hold values from -0.078125 to 0.078125
- mlp_out: bfloat16 [24576, 6144], P('row', 'col'), may hold values from -0.0390625 to 0.0390625
Outputs:
- purified: float32 [64, 28, 28, 3], P(('row', 'col'))
- encoded: bfloat16 [256, 6144], P('row', 'col')
The draws below stay inside these ranges and needn't reach their ends.
All inputs are finite; a program needn't handle non-finite values.
Results may differ from the reference program's by a relative error of at most 0.018.
Values may be sent and summed in bfloat16 or wider, within the bound.
A program may use at most 128 MiB of HBM per device.

```python
import math
import jax
import jax.numpy as jnp
from jax import lax

D = 6144
FF = 24576
CH = 256
PATCH = 14
SIDE = 28
IMAGES = 64


def draw_embed_weight(key, part):
    first, second = jax.random.split(jax.random.fold_in(key, 11))
    position = jnp.arange(D, dtype=jnp.float32) / D
    base = jax.random.normal(first, (PATCH * PATCH * 3, D), jnp.float32)
    trend = jnp.sqrt(0.5 + position)
    spread = 10.0 ** (jax.random.uniform(second, (D,), jnp.float32) - 1.0)
    column_scale = 2.0 * spread * trend / math.sqrt(PATCH * PATCH * 3)
    return (base * column_scale[None, :]).astype(jnp.bfloat16)


def draw_embed_bias(key, part):
    position = jnp.arange(D, dtype=jnp.float32) / D
    level = jax.random.uniform(jax.random.fold_in(key, 23), (D,), jnp.float32, 0.5, 1.5)
    trend = 0.5 + position
    return level * trend


def level_of(stream_key, shape, cuts, least, top_value):
    loudness, own = 1.0, jax.random.fold_in(stream_key, 6)
    for axis_at, blocks in cuts:
        heights = jnp.exp(jax.random.uniform(jax.random.fold_in(own, axis_at), (blocks,), jnp.float32, least / len(cuts), top_value / len(cuts)))
        loudness = loudness * jnp.repeat(heights, shape[axis_at] // blocks).reshape([-1 if axis == axis_at else 1 for axis in range(len(shape))])
    return loudness


def normal_values(key, extent, deviation, most, cuts=(), kind=jnp.bfloat16):
    drawn = deviation * jax.random.normal(key, extent, jnp.float32)
    if cuts:
        drawn = drawn * level_of(key, extent, cuts, -0.22, 0.18)
    return jnp.clip(drawn, -most, most).astype(kind)


def setup_inputs(seed: int = 0) -> dict:
    key_list = jax.random.split(jax.random.key(seed), 13)
    return {
        "images": normal_values(key_list[0], (IMAGES, SIDE, SIDE, 3), 1.0, 6.0, ((0, 32),), jnp.float32),
        "noise_field": normal_values(key_list[1], (IMAGES, SIDE, SIDE, 3), 1.0, 6.0, ((0, 32),), jnp.float32),
        "stem_weight": normal_values(key_list[2], (27, CH), 27 ** -0.5, 1.25),
        "level_one": normal_values(key_list[3], (4, 9 * CH, CH), (9 * CH) ** -0.5, 0.125),
        "down_weight": normal_values(key_list[4], (4 * CH, CH), (4 * CH) ** -0.5, 0.1875),
        "level_two": normal_values(key_list[5], (2, 9 * CH, CH), (9 * CH) ** -0.5, 0.125),
        "up_weight": normal_values(key_list[6], (CH, 4 * CH), CH ** -0.5, 0.375),
        "out_weight": normal_values(key_list[7], (CH, 3), CH ** -0.5, 0.375),
        "embed_weight": draw_embed_weight(jax.random.fold_in(key_list[12], 71), 0),
        "embed_bias": draw_embed_bias(jax.random.fold_in(key_list[12], 71), 0),
        "mlp_in": normal_values(key_list[10], (D, FF), D ** -0.5, 0.078125, ((0, 8), (1, 4))),
        "mlp_out": normal_values(key_list[11], (FF, D), FF ** -0.5, 0.0390625, ((0, 4), (1, 8))),
    }


step_size = 0.25
noise_gain = math.sqrt(0.5)
ln_epsilon = 1e-06

def neighbours(field):
    height = field.shape[1]
    breadth = field.shape[2]
    padded = jnp.pad(field, ((0, 0), (1, 1), (1, 1), (0, 0)))
    parts = [padded[:, row_off:row_off + height, col_off:col_off + breadth, :] for row_off in range(3) for col_off in range(3)]
    return jnp.concatenate(parts, axis=-1)

def project(field, weight):
    flat = field.reshape(-1, field.shape[-1])
    result = jnp.dot(flat, weight, preferred_element_type=jnp.float32)
    return result.reshape(field.shape[:-1] + (weight.shape[1],))

def convolve(field, kernel):
    return project(neighbours(field), kernel)

def activate(field):
    return jax.nn.gelu(field).astype(jnp.bfloat16)

def fold_pixels(field):
    count, height, breadth, depth = field.shape
    grouped = field.reshape(count, height // 2, 2, breadth // 2, 2, depth).transpose(0, 1, 3, 2, 4, 5)
    return grouped.reshape(count, height // 2, breadth // 2, 4 * depth)

def unfold_pixels(field, depth):
    count, height, breadth, _ = field.shape
    grouped = field.reshape(count, height, breadth, 2, 2, depth).transpose(0, 1, 3, 2, 4, 5)
    return grouped.reshape(count, 2 * height, 2 * breadth, depth)

def score_net(pixels, stem_weight, level_one, down_weight, level_two, up_weight, out_weight):
    stream = convolve(pixels.astype(jnp.bfloat16), stem_weight)
    for layer in range(2):
        stream = stream + convolve(activate(stream), level_one[layer])
    skipped = stream
    coarse = project(fold_pixels(stream.astype(jnp.bfloat16)), down_weight)
    for layer in range(2):
        coarse = coarse + convolve(activate(coarse), level_two[layer])
    lifted = project(coarse.astype(jnp.bfloat16), up_weight)
    stream = unfold_pixels(lifted, up_weight.shape[0]) + skipped
    for layer in range(2, 4):
        stream = stream + convolve(activate(stream), level_one[layer])
    return project(activate(stream), out_weight)

def patchify(pixels, patch_side):
    count, side = (pixels.shape[0], pixels.shape[1])
    grid = side // patch_side
    blocks = pixels.reshape(count, grid, patch_side, grid, patch_side, 3).transpose(0, 1, 3, 2, 4, 5)
    return blocks.reshape(count * grid * grid, patch_side * patch_side * 3)

def reference(images, noise_field, stem_weight, level_one, down_weight, level_two, up_weight, out_weight, embed_weight, embed_bias, mlp_in, mlp_out):

    def single_score(single):
        return score_net(single[None], stem_weight, level_one, down_weight, level_two, up_weight, out_weight)[0]
    score_field = lax.map(single_score, images)
    purified = images + step_size * score_field + noise_gain * noise_field
    patches = patchify(purified.astype(jnp.bfloat16), PATCH)
    embedded = (jnp.dot(patches, embed_weight, preferred_element_type=jnp.float32) + embed_bias).astype(jnp.bfloat16)
    values = embedded.astype(jnp.float32)
    row_mean = lax.optimization_barrier(jnp.mean(values, axis=1, keepdims=True))
    row_square = lax.optimization_barrier(jnp.mean(values * values, axis=1, keepdims=True))
    normed = ((values - row_mean) * lax.rsqrt(row_square - row_mean * row_mean + ln_epsilon)).astype(jnp.bfloat16)
    hidden = jax.nn.gelu(jnp.dot(normed, mlp_in, preferred_element_type=jnp.float32)).astype(jnp.bfloat16)
    encoded = (values + jnp.dot(hidden, mlp_out, preferred_element_type=jnp.float32)).astype(jnp.bfloat16)
    return (purified, encoded)
```

```python
import functools
import math

import jax
import jax.numpy as jnp
from jax import lax
from jax.experimental import pallas as pl
from jax.experimental.pallas import tpu as pltpu
from jax.sharding import PartitionSpec as P

PATCH = 14
SIDE = 28
WIDE = 32
HALF = 14
HWIDE = 16

step_size = 0.25
noise_gain = math.sqrt(0.5)
ln_epsilon = 1e-06
MESH = pl.DeviceIdType.MESH
MIB = 1024 * 1024
f32 = jnp.float32
bf16 = jnp.bfloat16


def dot(a, b):
    return jnp.dot(a, b, preferred_element_type=f32)


def remote(src, dst, send_sem, recv_sem, device):
    return pltpu.make_async_remote_copy(
        src_ref=src,
        dst_ref=dst,
        send_sem=send_sem,
        recv_sem=recv_sem,
        device_id=device,
        device_id_type=MESH,
    )


def masked_act(stream, wide, side):
    column = lax.broadcasted_iota(jnp.int32, stream.shape, 0) % wide
    return jnp.where(column < side, jax.nn.gelu(stream), 0.0)


def put_act(field, at, stream, wide, side):
    depth = stream.shape[1]
    rows = stream.shape[0]
    act = masked_act(stream, wide, side)
    field[pl.ds(at, rows), 0:depth] = pltpu.roll(act, 1, 0).astype(bf16)
    field[pl.ds(at, rows), depth : 2 * depth] = act.astype(bf16)
    field[pl.ds(at, rows), 2 * depth : 3 * depth] = pltpu.roll(act, rows - 1, 0).astype(bf16)


def conv_rows(field, weight, at, rows, wide):
    span = weight.shape[0] // 3
    total = None
    for row_off in range(3):
        part = dot(
            field[at + row_off * wide : at + row_off * wide + rows, :],
            weight[row_off * span : (row_off + 1) * span, :],
        )
        total = part if total is None else total + part
    return total


def score_kernel(
    pixels,
    noise,
    stem,
    level_one,
    down,
    level_two,
    up,
    out_t,
    mlp_in,
    mlp_out,
    purified,
    in_swapped,
    out_swapped,
    field_a,
    field_b,
    coarse_a,
    coarse_b,
    stream,
    halves,
    coarse,
    send_sem,
    recv_sem,
):
    col = lax.axis_index("col")
    core = col % 2
    sibling = {"col": col + 1 - 2 * core}
    barrier = pltpu.get_barrier_semaphore()
    pl.semaphore_signal(barrier, inc=1, device_id=sibling, device_id_type=MESH)
    pl.semaphore_wait(barrier, 1)
    width = mlp_in.shape[1] // 2
    height = mlp_out.shape[0] // 2
    swaps = [
        remote(
            mlp_in.at[:, pl.ds(pl.multiple_of((1 - core) * width, 128), width)],
            in_swapped,
            send_sem.at[0],
            recv_sem.at[0],
            sibling,
        ),
        remote(
            mlp_out.at[pl.ds(pl.multiple_of((1 - core) * height, 16), height), :],
            out_swapped,
            send_sem.at[1],
            recv_sem.at[1],
            sibling,
        ),
    ]
    for swap in swaps:
        swap.start()

    depth = stream.shape[1]
    cells = SIDE * WIDE
    ccells = HALF * HWIDE
    tile = 7 * WIDE
    for field, row, last in (
        (field_a, WIDE, cells),
        (field_b, WIDE, cells),
        (coarse_a, HWIDE, ccells),
        (coarse_b, HWIDE, ccells),
    ):
        field[0:row, :] = jnp.zeros((row, 3 * depth), bf16)
        field[row + last : row + last + row, :] = jnp.zeros((row, 3 * depth), bf16)

    def one_image(n, carry):
        view = pixels[n].astype(bf16).astype(f32)
        lanes = view.shape[1]
        groups = []
        for row_off in (-1, 0, 1):
            for col_off in (-1, 0, 1):
                shift = (-(row_off * WIDE + col_off)) % lanes
                groups.append(pltpu.roll(view, shift, 1) if shift else view)
        groups.extend([jnp.zeros_like(view)] * 7)
        columns = jnp.concatenate(groups, axis=0).T.astype(bf16)
        for at in range(0, cells, tile):
            now = dot(columns[at : at + tile, :], stem[...])
            stream[at : at + tile, :] = now
            put_act(field_a, WIDE + at, now, WIDE, SIDE)
        for at in range(0, cells, tile):
            now = stream[at : at + tile, :] + conv_rows(
                field_a, level_one.at[0], at, tile, WIDE
            )
            stream[at : at + tile, :] = now
            put_act(field_b, WIDE + at, now, WIDE, SIDE)
        for at in range(0, cells, tile):
            now = stream[at : at + tile, :] + conv_rows(
                field_b, level_one.at[1], at, tile, WIDE
            )
            stream[at : at + tile, :] = now
            for h in range(depth // 128):
                stream_halves[h][at : at + tile, :] = now[:, h * 128 : (h + 1) * 128]
        now = None
        for b in range(2):
            parts = [
                half[pl.ds(b, cells // 2, stride=2), :].astype(bf16).reshape(HALF, 2, HWIDE, 128)
                for half in stream_halves
            ]
            for a in range(2):
                piece = jnp.concatenate(
                    [part[:, a].reshape(ccells, 128) for part in parts], axis=1
                )
                at = (2 * a + b) * depth
                part = dot(piece, down[at : at + depth, :])
                now = part if now is None else now + part
        put_act(coarse_a, HWIDE, now, HWIDE, HALF)
        now = now + conv_rows(coarse_a, level_two.at[0], 0, ccells, HWIDE)
        put_act(coarse_b, HWIDE, now, HWIDE, HALF)
        now = now + conv_rows(coarse_b, level_two.at[1], 0, ccells, HWIDE)
        lifted = now.astype(bf16)
        for b in range(2):
            pieces = [
                dot(lifted, up[:, (2 * a + b) * depth : (2 * a + b + 1) * depth]).reshape(
                    HALF, 1, HWIDE, depth
                )
                for a in range(2)
            ]
            both = jnp.concatenate(pieces, axis=1).reshape(cells // 2, depth)
            for h in range(depth // 128):
                stream_halves[h][pl.ds(b, cells // 2, stride=2), :] = both[
                    :, h * 128 : (h + 1) * 128
                ]
        for at in range(0, cells, tile):
            now = stream[at : at + tile, :] + jnp.concatenate(
                [half[at : at + tile, :] for half in stream_halves], axis=1
            )
            stream[at : at + tile, :] = now
            put_act(field_a, WIDE + at, now, WIDE, SIDE)
        for at in range(0, cells, tile):
            now = stream[at : at + tile, :] + conv_rows(
                field_a, level_one.at[2], at, tile, WIDE
            )
            stream[at : at + tile, :] = now
            put_act(field_b, WIDE + at, now, WIDE, SIDE)
        for at in range(0, cells, tile):
            now = stream[at : at + tile, :] + conv_rows(
                field_b, level_one.at[3], at, tile, WIDE
            )
            coarse[at : at + tile, :] = jax.nn.gelu(now).astype(bf16)
        score = lax.dot_general(
            out_t[...], coarse[...], (((1,), (1,)), ((), ())), preferred_element_type=f32
        )
        purified[n] = (
            pixels[n] + step_size * score[0:8, :] + noise_gain * noise[n]
        )
        return carry

    stream_halves = [halves.at[h] for h in range(depth // 128)]
    coarse[cells:, :] = jnp.zeros((coarse.shape[0] - cells, depth), bf16)
    lax.fori_loop(0, pixels.shape[0], one_image, 0)
    for swap in swaps:
        swap.wait()


def run_score(pixels, noise, stem, level_one, down, level_two, up, out_t, mlp_in, mlp_out):
    depth = stem.shape[1]
    vmem = pl.BlockSpec(memory_space=pltpu.VMEM)
    anywhere = pl.BlockSpec(memory_space=pl.ANY)
    return pl.pallas_call(
        score_kernel,
        out_shape=(
            jax.ShapeDtypeStruct(pixels.shape, f32),
            jax.ShapeDtypeStruct((mlp_in.shape[0], mlp_in.shape[1] // 2), bf16),
            jax.ShapeDtypeStruct((mlp_out.shape[0] // 2, mlp_out.shape[1]), bf16),
        ),
        in_specs=[vmem] * 8 + [anywhere] * 2,
        out_specs=(vmem, anywhere, anywhere),
        scratch_shapes=[
            pltpu.VMEM(((SIDE + 2) * WIDE, 3 * depth), bf16),
            pltpu.VMEM(((SIDE + 2) * WIDE, 3 * depth), bf16),
            pltpu.VMEM(((HALF + 2) * HWIDE, 3 * depth), bf16),
            pltpu.VMEM(((HALF + 2) * HWIDE, 3 * depth), bf16),
            pltpu.VMEM((SIDE * WIDE, depth), f32),
            pltpu.VMEM((depth // 128, SIDE * WIDE, 128), f32),
            pltpu.VMEM((WIDE * WIDE, depth), bf16),
            pltpu.SemaphoreType.DMA((2,)),
            pltpu.SemaphoreType.DMA((2,)),
        ],
        compiler_params=pltpu.CompilerParams(
            collective_id=0, has_side_effects=True, vmem_limit_bytes=48 * MIB
        ),
        cost_estimate=pl.CostEstimate(
            flops=10_000_000_000, bytes_accessed=30_000_000, transcendentals=0
        ),
    )(pixels, noise, stem, level_one, down, level_two, up, out_t, mlp_in, mlp_out)


def mlp_kernel(
    rows,
    cols,
    chunk,
    patches,
    embed_weight,
    embed_bias,
    mlp_in,
    in_swapped,
    mlp_out,
    out_swapped,
    encoded,
    own_patches,
    row_patches,
    all_patches,
    embed_w,
    w_in,
    w_out,
    values,
    normed,
    partial_out,
    partial_in,
    hidden,
    total,
    pair_out,
    pair_in,
    last_out,
    last_in,
    load_sem,
    gather_send,
    gather_recv,
    spread_send,
    spread_recv,
    rs_send,
    rs_recv,
    ag_send,
    ag_recv,
    pair_sem,
    last_send,
    last_recv,
):
    row = lax.axis_index("row")
    col = lax.axis_index("col")
    z = col // 2
    core = col % 2
    depth = cols // 2
    last = depth - 1
    sibling = {"col": col + 1 - 2 * core}
    width = w_in.shape[2]
    height = w_out.shape[1]

    loads = [
        pltpu.make_async_copy(embed_weight, embed_w, load_sem.at[0]),
        pltpu.make_async_copy(
            mlp_in.at[:, pl.ds(pl.multiple_of(core * width, 128), width)],
            w_in.at[core],
            load_sem.at[1],
        ),
        pltpu.make_async_copy(in_swapped, w_in.at[1 - core], load_sem.at[2]),
        pltpu.make_async_copy(
            mlp_out.at[pl.ds(pl.multiple_of(core * height, 16), height), :],
            w_out.at[core],
            load_sem.at[3],
        ),
        pltpu.make_async_copy(out_swapped, w_out.at[1 - core], load_sem.at[4]),
    ]
    for load in loads:
        load.start()
    own_patches[...] = patches[...]

    barrier = pltpu.get_barrier_semaphore()
    for step in range(1, cols):
        pl.semaphore_signal(
            barrier, inc=1, device_id={"col": (col + step) % cols}, device_id_type=MESH
        )
    for step in range(1, rows):
        pl.semaphore_signal(
            barrier, inc=1, device_id={"row": (row + step) % rows}, device_id_type=MESH
        )
    pl.semaphore_wait(barrier, cols - 1 + rows - 1)

    gathers = [
        remote(
            own_patches,
            row_patches.at[col],
            gather_send.at[step],
            gather_recv.at[step],
            {"col": (col + step) % cols},
        )
        for step in range(1, cols)
    ]
    for gather in gathers:
        gather.start()
    row_patches[col] = own_patches[...]
    for gather in gathers:
        gather.wait_recv()
    per_row = row_patches.shape[0] * row_patches.shape[1]
    all_patches[row] = row_patches[...].reshape(per_row, row_patches.shape[2]).astype(bf16)
    spreads = [
        remote(
            all_patches.at[row],
            all_patches.at[row],
            spread_send.at[step],
            spread_recv.at[step],
            {"row": (row + step) % rows},
        )
        for step in range(1, rows)
    ]
    for spread in spreads:
        spread.start()
    loads[0].wait()
    for spread in spreads:
        spread.wait_recv()

    tokens = rows * per_row
    pixels = embed_w.shape[0]
    features = embed_w.shape[1]
    span = features // cols

    def embed(at):
        at = pl.multiple_of(at, 128)
        tokens_in = all_patches[...].reshape(tokens, all_patches.shape[2])[:, 0:pixels]
        return (
            (dot(tokens_in, embed_w[:, pl.ds(at, span)]) + embed_bias[0:1, pl.ds(at, span)])
            .astype(bf16)
            .astype(f32)
        )

    def add_statistics(step, sums):
        part = embed(step * span)
        return (
            sums[0] + jnp.sum(part, axis=1, keepdims=True),
            sums[1] + jnp.sum(part * part, axis=1, keepdims=True),
        )

    zeros = jnp.zeros((tokens, 1), f32)
    value_sums, square_sums = lax.fori_loop(0, cols, add_statistics, (zeros, zeros))
    mean = value_sums / features
    scale = lax.rsqrt(square_sums / features - mean * mean + ln_epsilon)
    for j in range(2):
        part = embed((2 * z + j) * span)
        values[j] = part
        normed[j] = ((part - mean) * scale).astype(bf16)
        total[j] = jnp.zeros((tokens, span), f32)
    for load in loads[1:]:
        load.wait()

    chunks = partial_out.shape[1]
    place = (z, last - z)
    ahead = ({"col": col + 2}, {"col": col - 2})
    behind = ({"col": col - 2}, {"col": col + 2})

    def rs_copy(d, i):
        return remote(
            partial_out.at[d, i], partial_in.at[d, i], rs_send.at[d, i], rs_recv.at[d, i], ahead[d]
        )

    def ag_copy(d, i):
        return remote(
            hidden.at[d, i], hidden.at[d, i], ag_send.at[d, i], ag_recv.at[d, i], behind[d]
        )

    def second(d, i):
        at = pl.multiple_of((d * chunks + i) * chunk, chunk)
        for j in range(2):
            total[j] += dot(hidden[d, i], w_out[j, pl.ds(at, chunk), :])

    def slot(t, carry):
        for d in range(2):
            i = t - place[d]

            @pl.when((i >= 0) & (i < chunks))
            def _():
                at = pl.multiple_of((d * chunks + i) * chunk, chunk)
                mine = dot(normed[0], w_in[0, :, pl.ds(at, chunk)]) + dot(
                    normed[1], w_in[1, :, pl.ds(at, chunk)]
                )

                @pl.when(place[d] == 0)
                def _():
                    partial_out[d, i] = mine.astype(bf16)

                @pl.when(place[d] > 0)
                def _():
                    rs_copy(d, i).wait_recv()
                    whole = mine + partial_in[d, i].astype(f32)

                    @pl.when(place[d] < last)
                    def _():
                        partial_out[d, i] = whole.astype(bf16)

                    @pl.when(place[d] == last)
                    def _():
                        hidden[d, i] = jax.nn.gelu(whole).astype(bf16)

                @pl.when(place[d] < last)
                def _():
                    rs_copy(d, i).start()

                @pl.when(place[d] == last)
                def _():
                    ag_copy(d, i).start()
                    second(d, i)

        for d in range(2):
            i = t - (2 * last - place[d])

            @pl.when((i >= 0) & (i < chunks) & (place[d] < last))
            def _():
                ag_copy(d, i).wait_recv()

                @pl.when(place[d] > 0)
                def _():
                    ag_copy(d, i).start()

                second(d, i)

        return carry

    lax.fori_loop(0, chunks + 2 * last, slot, 0)

    pair_out[...] = total[1 - core].astype(bf16)
    pair = remote(pair_out, pair_in, pair_sem.at[0], pair_sem.at[1], sibling)
    pair.start()
    pair.wait_recv()
    summed = total[core] + pair_in[...].astype(f32)
    last_out[...] = summed.astype(bf16).reshape(last_out.shape)
    finals = [
        remote(
            last_out.at[(row + step) % rows],
            last_in.at[step],
            last_send.at[step],
            last_recv.at[step],
            {"row": (row + step) % rows},
        )
        for step in range(1, rows)
    ]
    for final in finals:
        final.start()
    result = values[core, pl.ds(pl.multiple_of(row * per_row, 16), per_row), :]
    result = result + last_out[row].astype(f32)
    for step, final in enumerate(finals):
        final.wait_recv()
        result = result + last_in[step + 1].astype(f32)
    encoded[...] = result.astype(bf16)

    for copy in gathers + spreads + finals + [pair]:
        copy.wait_send()

    def drain(i, carry):
        for d in range(2):

            @pl.when(place[d] < last)
            def _():
                rs_copy(d, i).wait_send()

            @pl.when(place[d] > 0)
            def _():
                ag_copy(d, i).wait_send()

        return carry

    lax.fori_loop(0, chunks, drain, 0)


def run_mlp(
    rows, cols, patches, embed_weight, embed_bias, mlp_in, in_swapped, mlp_out, out_swapped
):
    per_device, pixels = patches.shape
    per_row = cols * per_device
    tokens = rows * per_row
    features = embed_weight.shape[1]
    span = features // cols
    width = in_swapped.shape[1]
    chunk = min(256, width // 2)
    chunks = width // 2 // chunk
    vmem = pl.BlockSpec(memory_space=pltpu.VMEM)
    anywhere = pl.BlockSpec(memory_space=pl.ANY)
    dma = pltpu.SemaphoreType.DMA
    return pl.pallas_call(
        functools.partial(mlp_kernel, rows, cols, chunk),
        out_shape=jax.ShapeDtypeStruct((per_row, span), bf16),
        in_specs=[vmem, anywhere, vmem, anywhere, anywhere, anywhere, anywhere],
        out_specs=vmem,
        scratch_shapes=[
            pltpu.VMEM((per_device, pixels), f32),
            pltpu.VMEM((cols, per_device, pixels), f32),
            pltpu.VMEM((rows, per_row, pixels), bf16),
            pltpu.VMEM(embed_weight.shape, bf16),
            pltpu.VMEM((2,) + in_swapped.shape, bf16),
            pltpu.VMEM((2,) + out_swapped.shape, bf16),
            pltpu.VMEM((2, tokens, span), f32),
            pltpu.VMEM((2, tokens, span), bf16),
            pltpu.VMEM((2, chunks, tokens, chunk), bf16),
            pltpu.VMEM((2, chunks, tokens, chunk), bf16),
            pltpu.VMEM((2, chunks, tokens, chunk), bf16),
            pltpu.VMEM((2, tokens, span), f32),
            pltpu.VMEM((tokens, span), bf16),
            pltpu.VMEM((tokens, span), bf16),
            pltpu.VMEM((rows, per_row, span), bf16),
            pltpu.VMEM((rows, per_row, span), bf16),
            dma((5,)),
            dma((cols,)),
            dma((cols,)),
            dma((rows,)),
            dma((rows,)),
            dma((2, chunks)),
            dma((2, chunks)),
            dma((2, chunks)),
            dma((2, chunks)),
            dma((2,)),
            dma((rows,)),
            dma((rows,)),
        ],
        compiler_params=pltpu.CompilerParams(
            collective_id=1, has_side_effects=True, vmem_limit_bytes=56 * MIB
        ),
        cost_estimate=pl.CostEstimate(
            flops=10_000_000_000, bytes_accessed=30_000_000, transcendentals=0
        ),
    )(patches, embed_weight, embed_bias, mlp_in, in_swapped, mlp_out, out_swapped)


def to_planes(field):
    moved = jnp.pad(
        field.transpose(0, 3, 1, 2), ((0, 0), (0, 5), (0, WIDE - SIDE), (0, WIDE - SIDE))
    )
    return moved.reshape(field.shape[0], 8, WIDE * WIDE)


def on_device(
    images,
    noise_field,
    stem_weight,
    level_one,
    down_weight,
    level_two,
    up_weight,
    out_weight,
    embed_weight,
    embed_bias,
    mlp_in,
    mlp_out,
):
    rows = lax.axis_size("row")
    cols = lax.axis_size("col")
    depth = stem_weight.shape[1]
    stem = jnp.pad(stem_weight.reshape(9, 3, depth), ((0, 7), (0, 5), (0, 0))).reshape(128, depth)
    out_t = jnp.pad(out_weight.T, ((0, 13), (0, 0)))
    planes, in_swapped, out_swapped = run_score(
        to_planes(images),
        to_planes(noise_field),
        stem,
        level_one,
        down_weight,
        level_two,
        up_weight,
        out_t,
        mlp_in,
        mlp_out,
    )
    count = images.shape[0]
    planes = planes.reshape(count, 8, WIDE, WIDE)[:, 0:3, 0:SIDE, 0:SIDE]
    purified = planes.transpose(0, 2, 3, 1)
    grid = SIDE // PATCH
    patches = planes.astype(bf16).reshape(count, 3, grid, PATCH, grid, PATCH)
    patches = patches.transpose(0, 2, 4, 3, 5, 1).reshape(count * grid * grid, PATCH * PATCH * 3)
    pixels = patches.shape[1]
    patches = jnp.pad(patches.astype(f32), ((0, 0), (0, -pixels % 128)))
    encoded = run_mlp(
        rows,
        cols,
        patches,
        embed_weight,
        embed_bias[None, :],
        mlp_in,
        in_swapped,
        mlp_out,
        out_swapped,
    )
    return (purified, encoded)


def solution(mesh):
    placed = (
        P(("row", "col"), None, None, None),
        P(("row", "col"), None, None, None),
        P(),
        P(),
        P(),
        P(),
        P(),
        P(),
        P(),
        P(),
        P("col", "row"),
        P("row", "col"),
    )
    return jax.shard_map(
        on_device,
        mesh=mesh,
        in_specs=placed,
        out_specs=(P(("row", "col"), None, None, None), P("row", "col")),
        check_vma=False,
    )
```

```python
import functools
import math

import jax
import jax.numpy as jnp
from jax import lax
from jax.experimental import pallas as pl
from jax.experimental.pallas import tpu as pltpu
from jax.sharding import PartitionSpec as P

PATCH = 14
SIDE = 28
WIDE = 32
HALF = 14
HWIDE = 16

step_size = 0.25
noise_gain = math.sqrt(0.5)
ln_epsilon = 1e-06
LAG = 2
MESH = pl.DeviceIdType.MESH
MIB = 1024 * 1024
f32 = jnp.float32
bf16 = jnp.bfloat16


def dot(a, b):
    return jnp.dot(a, b, preferred_element_type=f32)


def remote(src, dst, send_sem, recv_sem, device):
    return pltpu.make_async_remote_copy(
        src_ref=src,
        dst_ref=dst,
        send_sem=send_sem,
        recv_sem=recv_sem,
        device_id=device,
        device_id_type=MESH,
    )


def masked_act(stream, wide, side):
    column = lax.broadcasted_iota(jnp.int32, stream.shape, 0) % wide
    return jnp.where(column < side, jax.nn.gelu(stream), 0.0)


def put_act(field, at, stream, wide, side):
    depth = stream.shape[1]
    rows = stream.shape[0]
    act = masked_act(stream, wide, side)
    field[pl.ds(at, rows), 0:depth] = pltpu.roll(act, 1, 0).astype(bf16)
    field[pl.ds(at, rows), depth : 2 * depth] = act.astype(bf16)
    field[pl.ds(at, rows), 2 * depth : 3 * depth] = pltpu.roll(act, rows - 1, 0).astype(bf16)


def conv_rows(field, weight, at, rows, wide):
    span = weight.shape[0] // 3
    total = None
    for row_off in range(3):
        part = dot(
            field[at + row_off * wide : at + row_off * wide + rows, :],
            weight[row_off * span : (row_off + 1) * span, :],
        )
        total = part if total is None else total + part
    return total


def score_kernel(
    pixels,
    noise,
    stem,
    level_one_hbm,
    down_hbm,
    level_two_hbm,
    up_hbm,
    out_t,
    mlp_in,
    purified,
    in_swapped,
    level_one,
    down,
    level_two,
    up,
    field_a,
    field_b,
    coarse_a,
    coarse_b,
    stream,
    halves,
    coarse,
    load_sem,
    swap_sem,
):
    loads = [
        pltpu.make_async_copy(level_one_hbm.at[k], level_one.at[k], load_sem.at[k])
        for k in range(4)
    ]
    loads.append(pltpu.make_async_copy(down_hbm, down, load_sem.at[4]))
    loads.append(pltpu.make_async_copy(level_two_hbm, level_two, load_sem.at[5]))
    loads.append(pltpu.make_async_copy(up_hbm, up, load_sem.at[6]))
    for k in (0, 1, 4, 5, 6, 2, 3):
        loads[k].start()
    col = lax.axis_index("col")
    core = col % 2
    sibling = {"col": col + 1 - 2 * core}
    barrier = pltpu.get_barrier_semaphore()
    pl.semaphore_signal(barrier, inc=1, device_id=sibling, device_id_type=MESH)
    pl.semaphore_wait(barrier, 1)
    width = mlp_in.shape[1] // 2
    swap = remote(
        mlp_in.at[:, pl.ds(pl.multiple_of((1 - core) * width, 128), width)],
        in_swapped,
        swap_sem.at[0],
        swap_sem.at[1],
        sibling,
    )
    swap.start()

    depth = stream.shape[1]
    cells = SIDE * WIDE
    ccells = HALF * HWIDE
    tile = 7 * WIDE
    for field, row, last in (
        (field_a, WIDE, cells),
        (field_b, WIDE, cells),
        (coarse_a, HWIDE, ccells),
        (coarse_b, HWIDE, ccells),
    ):
        field[0:row, :] = jnp.zeros((row, 3 * depth), bf16)
        field[row + last : row + last + row, :] = jnp.zeros((row, 3 * depth), bf16)

    def one_image(n, carry):
        def arrived(*which):
            @pl.when(n == 0)
            def _():
                for k in which:
                    loads[k].wait()

        view = pixels[n].astype(bf16).astype(f32)
        lanes = view.shape[1]
        groups = []
        for row_off in (-1, 0, 1):
            for col_off in (-1, 0, 1):
                shift = (-(row_off * WIDE + col_off)) % lanes
                groups.append(pltpu.roll(view, shift, 1) if shift else view)
        groups.extend([jnp.zeros_like(view)] * 7)
        columns = jnp.concatenate(groups, axis=0).T.astype(bf16)
        for at in range(0, cells, tile):
            now = dot(columns[at : at + tile, :], stem[...])
            stream[at : at + tile, :] = now
            put_act(field_a, WIDE + at, now, WIDE, SIDE)
        arrived(0)
        for at in range(0, cells, tile):
            now = stream[at : at + tile, :] + conv_rows(
                field_a, level_one.at[0], at, tile, WIDE
            )
            stream[at : at + tile, :] = now
            put_act(field_b, WIDE + at, now, WIDE, SIDE)
        arrived(1)
        for at in range(0, cells, tile):
            now = stream[at : at + tile, :] + conv_rows(
                field_b, level_one.at[1], at, tile, WIDE
            )
            stream[at : at + tile, :] = now
            for h in range(depth // 128):
                stream_halves[h][at : at + tile, :] = now[:, h * 128 : (h + 1) * 128]
        arrived(4, 5, 6)
        now = None
        for b in range(2):
            parts = [
                half[pl.ds(b, cells // 2, stride=2), :].astype(bf16).reshape(HALF, 2, HWIDE, 128)
                for half in stream_halves
            ]
            for a in range(2):
                piece = jnp.concatenate(
                    [part[:, a].reshape(ccells, 128) for part in parts], axis=1
                )
                at = (2 * a + b) * depth
                part = dot(piece, down[at : at + depth, :])
                now = part if now is None else now + part
        put_act(coarse_a, HWIDE, now, HWIDE, HALF)
        now = now + conv_rows(coarse_a, level_two.at[0], 0, ccells, HWIDE)
        put_act(coarse_b, HWIDE, now, HWIDE, HALF)
        now = now + conv_rows(coarse_b, level_two.at[1], 0, ccells, HWIDE)
        lifted = now.astype(bf16)
        for b in range(2):
            pieces = [
                dot(lifted, up[:, (2 * a + b) * depth : (2 * a + b + 1) * depth]).reshape(
                    HALF, 1, HWIDE, depth
                )
                for a in range(2)
            ]
            both = jnp.concatenate(pieces, axis=1).reshape(cells // 2, depth)
            for h in range(depth // 128):
                stream_halves[h][pl.ds(b, cells // 2, stride=2), :] = both[
                    :, h * 128 : (h + 1) * 128
                ]
        for at in range(0, cells, tile):
            now = stream[at : at + tile, :] + jnp.concatenate(
                [half[at : at + tile, :] for half in stream_halves], axis=1
            )
            stream[at : at + tile, :] = now
            put_act(field_a, WIDE + at, now, WIDE, SIDE)
        arrived(2, 3)
        for at in range(0, cells, tile):
            now = stream[at : at + tile, :] + conv_rows(
                field_a, level_one.at[2], at, tile, WIDE
            )
            stream[at : at + tile, :] = now
            put_act(field_b, WIDE + at, now, WIDE, SIDE)
        for at in range(0, cells, tile):
            now = stream[at : at + tile, :] + conv_rows(
                field_b, level_one.at[3], at, tile, WIDE
            )
            coarse[at : at + tile, :] = jax.nn.gelu(now).astype(bf16)
        score = lax.dot_general(
            out_t[...], coarse[...], (((1,), (1,)), ((), ())), preferred_element_type=f32
        )
        purified[n] = (
            pixels[n] + step_size * score[0:8, :] + noise_gain * noise[n]
        )
        return carry

    stream_halves = [halves.at[h] for h in range(depth // 128)]
    coarse[cells:, :] = jnp.zeros((coarse.shape[0] - cells, depth), bf16)
    lax.fori_loop(0, pixels.shape[0], one_image, 0)
    swap.wait()


def run_score(pixels, noise, stem, level_one, down, level_two, up, out_t, mlp_in):
    depth = stem.shape[1]
    vmem = pl.BlockSpec(memory_space=pltpu.VMEM)
    anywhere = pl.BlockSpec(memory_space=pl.ANY)
    return pl.pallas_call(
        score_kernel,
        out_shape=(
            jax.ShapeDtypeStruct(pixels.shape, f32),
            jax.ShapeDtypeStruct((mlp_in.shape[0], mlp_in.shape[1] // 2), bf16),
        ),
        in_specs=[vmem] * 3 + [anywhere] * 4 + [vmem, anywhere],
        out_specs=(vmem, anywhere),
        scratch_shapes=[
            pltpu.VMEM(level_one.shape, bf16),
            pltpu.VMEM(down.shape, bf16),
            pltpu.VMEM(level_two.shape, bf16),
            pltpu.VMEM(up.shape, bf16),
            pltpu.VMEM(((SIDE + 2) * WIDE, 3 * depth), bf16),
            pltpu.VMEM(((SIDE + 2) * WIDE, 3 * depth), bf16),
            pltpu.VMEM(((HALF + 2) * HWIDE, 3 * depth), bf16),
            pltpu.VMEM(((HALF + 2) * HWIDE, 3 * depth), bf16),
            pltpu.VMEM((SIDE * WIDE, depth), f32),
            pltpu.VMEM((depth // 128, SIDE * WIDE, 128), f32),
            pltpu.VMEM((WIDE * WIDE, depth), bf16),
            pltpu.SemaphoreType.DMA((7,)),
            pltpu.SemaphoreType.DMA((2,)),
        ],
        compiler_params=pltpu.CompilerParams(
            collective_id=0, has_side_effects=True, vmem_limit_bytes=60 * MIB
        ),
        cost_estimate=pl.CostEstimate(
            flops=10_000_000_000, bytes_accessed=30_000_000, transcendentals=0
        ),
    )(pixels, noise, stem, level_one, down, level_two, up, out_t, mlp_in)


def mlp_kernel(
    rows,
    cols,
    chunk,
    patches,
    embed_weight,
    embed_bias,
    mlp_in,
    in_swapped,
    mlp_out,
    encoded,
    own_patches,
    row_patches,
    all_patches,
    embed_w,
    w_in,
    w_out,
    w_other,
    values,
    normed,
    mine,
    partial_out,
    partial_in,
    hidden,
    total,
    pair_out,
    pair_in,
    last_out,
    last_in,
    load_sem,
    gather_send,
    gather_recv,
    spread_send,
    spread_recv,
    rs_send,
    rs_recv,
    ag_send,
    ag_recv,
    swap_sem,
    pair_send,
    pair_recv,
    last_send,
    last_recv,
):
    row = lax.axis_index("row")
    col = lax.axis_index("col")
    z = col // 2
    core = col % 2
    depth = cols // 2
    last = depth - 1
    sibling = {"col": col + 1 - 2 * core}
    width = w_in.shape[2]
    height = w_out.shape[0]

    loads = [
        pltpu.make_async_copy(embed_weight, embed_w, load_sem.at[0]),
        pltpu.make_async_copy(
            mlp_in.at[:, pl.ds(pl.multiple_of(core * width, 128), width)],
            w_in.at[core],
            load_sem.at[1],
        ),
        pltpu.make_async_copy(in_swapped, w_in.at[1 - core], load_sem.at[2]),
        pltpu.make_async_copy(
            mlp_out.at[pl.ds(pl.multiple_of(core * height, 16), height), :],
            w_out,
            load_sem.at[3],
        ),
    ]
    for load in loads:
        load.start()
    own_patches[...] = patches[...]

    barrier = pltpu.get_barrier_semaphore()
    for step in range(1, cols):
        pl.semaphore_signal(
            barrier, inc=1, device_id={"col": (col + step) % cols}, device_id_type=MESH
        )
    for step in range(1, rows):
        pl.semaphore_signal(
            barrier, inc=1, device_id={"row": (row + step) % rows}, device_id_type=MESH
        )
    pl.semaphore_wait(barrier, cols - 1 + rows - 1)

    gathers = [
        remote(
            own_patches,
            row_patches.at[col],
            gather_send.at[step],
            gather_recv.at[step],
            {"col": (col + step) % cols},
        )
        for step in range(1, cols)
    ]
    for gather in gathers:
        gather.start()
    row_patches[col] = own_patches[...]
    for gather in gathers:
        gather.wait_recv()
    per_row = row_patches.shape[0] * row_patches.shape[1]
    all_patches[row] = row_patches[...].reshape(per_row, row_patches.shape[2]).astype(bf16)
    spreads = [
        remote(
            all_patches.at[row],
            all_patches.at[row],
            spread_send.at[step],
            spread_recv.at[step],
            {"row": (row + step) % rows},
        )
        for step in range(1, rows)
    ]
    for spread in spreads:
        spread.start()
    loads[0].wait()
    for spread in spreads:
        spread.wait_recv()
    swap = remote(
        mlp_out.at[pl.ds(pl.multiple_of((1 - core) * height, 16), height), :],
        w_other,
        swap_sem.at[0],
        swap_sem.at[1],
        sibling,
    )
    swap.start()

    tokens = rows * per_row
    pixels = embed_w.shape[0]
    features = embed_w.shape[1]
    span = features // cols

    def embed(at):
        at = pl.multiple_of(at, 128)
        tokens_in = all_patches[...].reshape(tokens, all_patches.shape[2])[:, 0:pixels]
        return (
            (dot(tokens_in, embed_w[:, pl.ds(at, span)]) + embed_bias[0:1, pl.ds(at, span)])
            .astype(bf16)
            .astype(f32)
        )

    def add_statistics(step, sums):
        part = embed(step * span)
        return (
            sums[0] + jnp.sum(part, axis=1, keepdims=True),
            sums[1] + jnp.sum(part * part, axis=1, keepdims=True),
        )

    zeros = jnp.zeros((tokens, 1), f32)
    value_sums, square_sums = lax.fori_loop(0, cols, add_statistics, (zeros, zeros))
    mean = value_sums / features
    scale = lax.rsqrt(square_sums / features - mean * mean + ln_epsilon)
    for j in range(2):
        part = embed((2 * z + j) * span)
        values[j] = part
        normed[j] = ((part - mean) * scale).astype(bf16)
        total[j] = jnp.zeros((tokens, span), f32)
    loads[1].wait()
    loads[2].wait()

    chunks = partial_out.shape[1]
    place = (z, last - z)
    ahead = ({"col": col + 2}, {"col": col - 2})
    behind = ({"col": col - 2}, {"col": col + 2})

    def rs_copy(d, i):
        return remote(
            partial_out.at[d, i], partial_in.at[d, i], rs_send.at[d, i], rs_recv.at[d, i], ahead[d]
        )

    def ag_copy(d, i):
        return remote(
            hidden.at[d, i], hidden.at[d, i], ag_send.at[d, i], ag_recv.at[d, i], behind[d]
        )

    def slot(t, carry):
        @pl.when(t == LAG * last)
        def _():
            loads[3].wait()
            swap.wait_recv()

        for d in range(2):
            i = t - LAG * (2 * last - place[d])

            @pl.when((i >= 0) & (i < chunks) & (place[d] < last))
            def _():
                ag_copy(d, i).wait_recv()

                @pl.when(place[d] > 0)
                def _():
                    ag_copy(d, i).start()

        for d in range(2):
            i = t - LAG * place[d]

            @pl.when((i >= 0) & (i < chunks))
            def _():
                @pl.when(i % 2 == 0)
                def _():
                    at = pl.multiple_of((d * chunks + i) * chunk, 2 * chunk)
                    both = dot(normed[0], w_in[0, :, pl.ds(at, 2 * chunk)]) + dot(
                        normed[1], w_in[1, :, pl.ds(at, 2 * chunk)]
                    )
                    mine[d, 0] = both[:, 0:chunk]
                    mine[d, 1] = both[:, chunk : 2 * chunk]

                @pl.when(place[d] == 0)
                def _():
                    partial_out[d, i] = mine[d, i % 2].astype(bf16)

                @pl.when(place[d] > 0)
                def _():
                    rs_copy(d, i).wait_recv()
                    whole = mine[d, i % 2] + partial_in[d, i].astype(f32)

                    @pl.when(place[d] < last)
                    def _():
                        partial_out[d, i] = whole.astype(bf16)

                    @pl.when(place[d] == last)
                    def _():
                        hidden[d, i] = jax.nn.gelu(whole).astype(bf16)

                @pl.when(place[d] < last)
                def _():
                    rs_copy(d, i).start()

                @pl.when(place[d] == last)
                def _():
                    ag_copy(d, i).start()

        for d in range(2):
            i = t - LAG * (2 * last - place[d])

            @pl.when((i >= 0) & (i < chunks) & (i % 2 == 1))
            def _():
                at = pl.multiple_of((d * chunks + i - 1) * chunk, 2 * chunk)
                units = jnp.concatenate([hidden[d, i - 1], hidden[d, i]], axis=1)
                total[0] += dot(units, w_out[pl.ds(at, 2 * chunk), :])
                total[1] += dot(units, w_other[pl.ds(at, 2 * chunk), :])

        return carry

    lax.fori_loop(0, chunks + 2 * LAG * last, slot, 0)

    pairs, finals = [], []
    for step in list(range(1, rows)) + [0]:
        block = (row + step) % rows
        at = pl.ds(pl.multiple_of(block * per_row, 16), per_row)
        pair_out[step] = total[1, at, :].astype(bf16)
        pair = remote(
            pair_out.at[step], pair_in.at[step], pair_send.at[step], pair_recv.at[step], sibling
        )
        pair.start()
        pairs.append(pair)
    for step in list(range(1, rows)) + [0]:
        block = (row + step) % rows
        at = pl.ds(pl.multiple_of(block * per_row, 16), per_row)
        pairs[step - 1].wait_recv()
        summed = total[0, at, :] + pair_in[step].astype(f32)
        if step == 0:
            result = values[core, at, :] + summed
        else:
            last_out[step] = summed.astype(bf16)
            final = remote(
                last_out.at[step],
                last_in.at[step],
                last_send.at[step],
                last_recv.at[step],
                {"row": block},
            )
            final.start()
            finals.append(final)
    for step, final in enumerate(finals):
        final.wait_recv()
        result = result + last_in[step + 1].astype(f32)
    encoded[...] = result.astype(bf16)

    for copy in gathers + spreads + finals + pairs + [swap]:
        copy.wait_send()

    def drain(i, carry):
        for d in range(2):

            @pl.when(place[d] < last)
            def _():
                rs_copy(d, i).wait_send()

            @pl.when(place[d] > 0)
            def _():
                ag_copy(d, i).wait_send()

        return carry

    lax.fori_loop(0, chunks, drain, 0)


def run_mlp(
    rows, cols, patches, embed_weight, embed_bias, mlp_in, in_swapped, mlp_out
):
    per_device, pixels = patches.shape
    per_row = cols * per_device
    tokens = rows * per_row
    features = embed_weight.shape[1]
    span = features // cols
    width = in_swapped.shape[1]
    chunk = min(128, width // 2)
    chunks = width // 2 // chunk
    vmem = pl.BlockSpec(memory_space=pltpu.VMEM)
    anywhere = pl.BlockSpec(memory_space=pl.ANY)
    dma = pltpu.SemaphoreType.DMA
    return pl.pallas_call(
        functools.partial(mlp_kernel, rows, cols, chunk),
        out_shape=jax.ShapeDtypeStruct((per_row, span), bf16),
        in_specs=[vmem, anywhere, vmem, anywhere, anywhere, anywhere],
        out_specs=vmem,
        scratch_shapes=[
            pltpu.VMEM((per_device, pixels), f32),
            pltpu.VMEM((cols, per_device, pixels), f32),
            pltpu.VMEM((rows, per_row, pixels), bf16),
            pltpu.VMEM(embed_weight.shape, bf16),
            pltpu.VMEM((2,) + in_swapped.shape, bf16),
            pltpu.VMEM((width, span), bf16),
            pltpu.VMEM((width, span), bf16),
            pltpu.VMEM((2, tokens, span), f32),
            pltpu.VMEM((2, tokens, span), bf16),
            pltpu.VMEM((2, 2, tokens, chunk), f32),
            pltpu.VMEM((2, chunks, tokens, chunk), bf16),
            pltpu.VMEM((2, chunks, tokens, chunk), bf16),
            pltpu.VMEM((2, chunks, tokens, chunk), bf16),
            pltpu.VMEM((2, tokens, span), f32),
            pltpu.VMEM((rows, per_row, span), bf16),
            pltpu.VMEM((rows, per_row, span), bf16),
            pltpu.VMEM((rows, per_row, span), bf16),
            pltpu.VMEM((rows, per_row, span), bf16),
            dma((4,)),
            dma((cols,)),
            dma((cols,)),
            dma((rows,)),
            dma((rows,)),
            dma((2, chunks)),
            dma((2, chunks)),
            dma((2, chunks)),
            dma((2, chunks)),
            dma((2,)),
            dma((rows,)),
            dma((rows,)),
            dma((rows,)),
            dma((rows,)),
        ],
        compiler_params=pltpu.CompilerParams(
            collective_id=1, has_side_effects=True, vmem_limit_bytes=56 * MIB
        ),
        cost_estimate=pl.CostEstimate(
            flops=10_000_000_000, bytes_accessed=30_000_000, transcendentals=0
        ),
    )(patches, embed_weight, embed_bias, mlp_in, in_swapped, mlp_out)


def to_planes(field):
    moved = jnp.pad(
        field.transpose(0, 3, 1, 2), ((0, 0), (0, 5), (0, WIDE - SIDE), (0, WIDE - SIDE))
    )
    return moved.reshape(field.shape[0], 8, WIDE * WIDE)


def on_device(
    images,
    noise_field,
    stem_weight,
    level_one,
    down_weight,
    level_two,
    up_weight,
    out_weight,
    embed_weight,
    embed_bias,
    mlp_in,
    mlp_out,
):
    rows = lax.axis_size("row")
    cols = lax.axis_size("col")
    depth = stem_weight.shape[1]
    stem = jnp.pad(stem_weight.reshape(9, 3, depth), ((0, 7), (0, 5), (0, 0))).reshape(128, depth)
    out_t = jnp.pad(out_weight.T, ((0, 13), (0, 0)))
    planes, in_swapped = run_score(
        to_planes(images),
        to_planes(noise_field),
        stem,
        level_one,
        down_weight,
        level_two,
        up_weight,
        out_t,
        mlp_in,
    )
    count = images.shape[0]
    planes = planes.reshape(count, 8, WIDE, WIDE)[:, 0:3, 0:SIDE, 0:SIDE]
    purified = planes.transpose(0, 2, 3, 1)
    grid = SIDE // PATCH
    patches = planes.astype(bf16).reshape(count, 3, grid, PATCH, grid, PATCH)
    patches = patches.transpose(0, 2, 4, 3, 5, 1).reshape(count * grid * grid, PATCH * PATCH * 3)
    pixels = patches.shape[1]
    patches = jnp.pad(patches.astype(f32), ((0, 0), (0, -pixels % 128)))
    encoded = run_mlp(
        rows,
        cols,
        patches,
        embed_weight,
        embed_bias[None, :],
        mlp_in,
        in_swapped,
        mlp_out,
    )
    return (purified, encoded)


def solution(mesh):
    placed = (
        P(("row", "col"), None, None, None),
        P(("row", "col"), None, None, None),
        P(),
        P(),
        P(),
        P(),
        P(),
        P(),
        P(),
        P(),
        P("col", "row"),
        P("row", "col"),
    )
    return jax.shard_map(
        on_device,
        mesh=mesh,
        in_specs=placed,
        out_specs=(P(("row", "col"), None, None, None), P("row", "col")),
        check_vma=False,
    )
```

```python
import functools
import math

import jax
import jax.numpy as jnp
from jax import lax
from jax.experimental import pallas as pl
from jax.experimental.pallas import tpu as pltpu
from jax.sharding import PartitionSpec as P

PATCH = 14
SIDE = 28
WIDE = 32
HALF = 14
HWIDE = 16

step_size = 0.25
noise_gain = math.sqrt(0.5)
ln_epsilon = 1e-06
LAG = 2
MESH = pl.DeviceIdType.MESH
MIB = 1024 * 1024
f32 = jnp.float32
bf16 = jnp.bfloat16


def dot(a, b):
    return jnp.dot(a, b, preferred_element_type=f32)


def remote(src, dst, send_sem, recv_sem, device):
    return pltpu.make_async_remote_copy(
        src_ref=src,
        dst_ref=dst,
        send_sem=send_sem,
        recv_sem=recv_sem,
        device_id=device,
        device_id_type=MESH,
    )


def masked_act(stream, wide, side):
    column = lax.broadcasted_iota(jnp.int32, stream.shape, 0) % wide
    return jnp.where(column < side, jax.nn.gelu(stream), 0.0)


def put_act(field, at, stream, wide, side):
    depth = stream.shape[1]
    rows = stream.shape[0]
    act = masked_act(stream, wide, side)
    field[pl.ds(at, rows), 0:depth] = pltpu.roll(act, 1, 0).astype(bf16)
    field[pl.ds(at, rows), depth : 2 * depth] = act.astype(bf16)
    field[pl.ds(at, rows), 2 * depth : 3 * depth] = pltpu.roll(act, rows - 1, 0).astype(bf16)


def conv_rows(field, weight, at, rows, wide):
    span = weight.shape[0] // 3
    total = None
    for row_off in range(3):
        part = dot(
            field[at + row_off * wide : at + row_off * wide + rows, :],
            weight[row_off * span : (row_off + 1) * span, :],
        )
        total = part if total is None else total + part
    return total


def score_kernel(
    images,
    noise_field,
    stem_weight,
    level_one_hbm,
    down_hbm,
    level_two_hbm,
    up_hbm,
    out_t,
    mlp_in,
    purified,
    in_swapped,
    pixels,
    noise,
    result,
    stem,
    level_one,
    down,
    level_two,
    up,
    field_a,
    field_b,
    coarse_a,
    coarse_b,
    stream,
    halves,
    coarse,
    load_sem,
    swap_sem,
):
    loads = [
        pltpu.make_async_copy(level_one_hbm.at[k], level_one.at[k], load_sem.at[k])
        for k in range(4)
    ]
    loads.append(pltpu.make_async_copy(down_hbm, down, load_sem.at[4]))
    loads.append(pltpu.make_async_copy(level_two_hbm, level_two, load_sem.at[5]))
    loads.append(pltpu.make_async_copy(up_hbm, up, load_sem.at[6]))
    for k in (0, 1, 4, 5, 6, 2, 3):
        loads[k].start()
    col = lax.axis_index("col")
    core = col % 2
    sibling = {"col": col + 1 - 2 * core}
    barrier = pltpu.get_barrier_semaphore()
    pl.semaphore_signal(barrier, inc=1, device_id=sibling, device_id_type=MESH)
    pl.semaphore_wait(barrier, 1)
    width = mlp_in.shape[1] // 2
    swap = remote(
        mlp_in.at[:, pl.ds(pl.multiple_of((1 - core) * width, 128), width)],
        in_swapped,
        swap_sem.at[0],
        swap_sem.at[1],
        sibling,
    )
    swap.start()

    depth = stream.shape[1]
    count = pixels.shape[0]
    for planes, given in ((pixels, images), (noise, noise_field)):
        planes[...] = jnp.zeros(planes.shape, f32)
        for n in range(count):
            for y in range(SIDE):
                planes[n, 0:3, y * WIDE : y * WIDE + SIDE] = given[y, :, n, :]
    stem[...] = jnp.zeros(stem.shape, f32)
    stem_rows = stem_weight[...].astype(f32)
    for g in range(9):
        stem[8 * g : 8 * g + 3, :] = stem_rows[3 * g : 3 * g + 3, :]
    cells = SIDE * WIDE
    ccells = HALF * HWIDE
    tile = 7 * WIDE
    for field, row, last in (
        (field_a, WIDE, cells),
        (field_b, WIDE, cells),
        (coarse_a, HWIDE, ccells),
        (coarse_b, HWIDE, ccells),
    ):
        field[0:row, :] = jnp.zeros((row, 3 * depth), bf16)
        field[row + last : row + last + row, :] = jnp.zeros((row, 3 * depth), bf16)

    def one_image(n, carry):
        def arrived(*which):
            @pl.when(n == 0)
            def _():
                for k in which:
                    loads[k].wait()

        view = pixels[n].astype(bf16).astype(f32)
        lanes = view.shape[1]
        groups = []
        for row_off in (-1, 0, 1):
            for col_off in (-1, 0, 1):
                shift = (-(row_off * WIDE + col_off)) % lanes
                groups.append(pltpu.roll(view, shift, 1) if shift else view)
        groups.extend([jnp.zeros_like(view)] * 7)
        columns = jnp.concatenate(groups, axis=0).T.astype(bf16)
        for at in range(0, cells, tile):
            now = dot(columns[at : at + tile, :], stem[...].astype(bf16))
            stream[at : at + tile, :] = now
            put_act(field_a, WIDE + at, now, WIDE, SIDE)
        arrived(0)
        for at in range(0, cells, tile):
            now = stream[at : at + tile, :] + conv_rows(
                field_a, level_one.at[0], at, tile, WIDE
            )
            stream[at : at + tile, :] = now
            put_act(field_b, WIDE + at, now, WIDE, SIDE)
        arrived(1)
        for at in range(0, cells, tile):
            now = stream[at : at + tile, :] + conv_rows(
                field_b, level_one.at[1], at, tile, WIDE
            )
            stream[at : at + tile, :] = now
            for h in range(depth // 128):
                stream_halves[h][at : at + tile, :] = now[:, h * 128 : (h + 1) * 128]
        arrived(4, 5, 6)
        now = None
        for b in range(2):
            parts = [
                half[pl.ds(b, cells // 2, stride=2), :].astype(bf16).reshape(HALF, 2, HWIDE, 128)
                for half in stream_halves
            ]
            for a in range(2):
                piece = jnp.concatenate(
                    [part[:, a].reshape(ccells, 128) for part in parts], axis=1
                )
                at = (2 * a + b) * depth
                part = dot(piece, down[at : at + depth, :])
                now = part if now is None else now + part
        put_act(coarse_a, HWIDE, now, HWIDE, HALF)
        now = now + conv_rows(coarse_a, level_two.at[0], 0, ccells, HWIDE)
        put_act(coarse_b, HWIDE, now, HWIDE, HALF)
        now = now + conv_rows(coarse_b, level_two.at[1], 0, ccells, HWIDE)
        lifted = now.astype(bf16)
        for b in range(2):
            pieces = [
                dot(lifted, up[:, (2 * a + b) * depth : (2 * a + b + 1) * depth]).reshape(
                    HALF, 1, HWIDE, depth
                )
                for a in range(2)
            ]
            both = jnp.concatenate(pieces, axis=1).reshape(cells // 2, depth)
            for h in range(depth // 128):
                stream_halves[h][pl.ds(b, cells // 2, stride=2), :] = both[
                    :, h * 128 : (h + 1) * 128
                ]
        for at in range(0, cells, tile):
            now = stream[at : at + tile, :] + jnp.concatenate(
                [half[at : at + tile, :] for half in stream_halves], axis=1
            )
            stream[at : at + tile, :] = now
            put_act(field_a, WIDE + at, now, WIDE, SIDE)
        arrived(2, 3)
        for at in range(0, cells, tile):
            now = stream[at : at + tile, :] + conv_rows(
                field_a, level_one.at[2], at, tile, WIDE
            )
            stream[at : at + tile, :] = now
            put_act(field_b, WIDE + at, now, WIDE, SIDE)
        for at in range(0, cells, tile):
            now = stream[at : at + tile, :] + conv_rows(
                field_b, level_one.at[3], at, tile, WIDE
            )
            coarse[at : at + tile, :] = jax.nn.gelu(now).astype(bf16)
        score = lax.dot_general(
            out_t[...], coarse[...], (((1,), (1,)), ((), ())), preferred_element_type=f32
        )
        result[n, 0:3, :] = (
            pixels[n, 0:3, :] + step_size * score + noise_gain * noise[n, 0:3, :]
        )
        return carry

    stream_halves = [halves.at[h] for h in range(depth // 128)]
    coarse[cells:, :] = jnp.zeros((coarse.shape[0] - cells, depth), bf16)
    lax.fori_loop(0, count, one_image, 0)
    for n in range(count):
        for y in range(SIDE):
            purified[y, :, n, :] = result[n, 0:3, y * WIDE : y * WIDE + SIDE]
    swap.wait()


def run_score(images, noise_field, stem, level_one, down, level_two, up, out_t, mlp_in):
    depth = stem.shape[1]
    vmem = pl.BlockSpec(memory_space=pltpu.VMEM)
    anywhere = pl.BlockSpec(memory_space=pl.ANY)
    return pl.pallas_call(
        score_kernel,
        out_shape=(
            jax.ShapeDtypeStruct(images.shape, f32),
            jax.ShapeDtypeStruct((mlp_in.shape[0], mlp_in.shape[1] // 2), bf16),
        ),
        in_specs=[vmem] * 3 + [anywhere] * 4 + [vmem, anywhere],
        out_specs=(vmem, anywhere),
        scratch_shapes=[
            pltpu.VMEM((images.shape[2], 8, WIDE * WIDE), f32),
            pltpu.VMEM((images.shape[2], 8, WIDE * WIDE), f32),
            pltpu.VMEM((images.shape[2], 8, WIDE * WIDE), f32),
            pltpu.VMEM((128, depth), f32),
            pltpu.VMEM(level_one.shape, bf16),
            pltpu.VMEM(down.shape, bf16),
            pltpu.VMEM(level_two.shape, bf16),
            pltpu.VMEM(up.shape, bf16),
            pltpu.VMEM(((SIDE + 2) * WIDE, 3 * depth), bf16),
            pltpu.VMEM(((SIDE + 2) * WIDE, 3 * depth), bf16),
            pltpu.VMEM(((HALF + 2) * HWIDE, 3 * depth), bf16),
            pltpu.VMEM(((HALF + 2) * HWIDE, 3 * depth), bf16),
            pltpu.VMEM((SIDE * WIDE, depth), f32),
            pltpu.VMEM((depth // 128, SIDE * WIDE, 128), f32),
            pltpu.VMEM((WIDE * WIDE, depth), bf16),
            pltpu.SemaphoreType.DMA((7,)),
            pltpu.SemaphoreType.DMA((2,)),
        ],
        compiler_params=pltpu.CompilerParams(
            collective_id=0, has_side_effects=True, vmem_limit_bytes=60 * MIB
        ),
        cost_estimate=pl.CostEstimate(
            flops=10_000_000_000, bytes_accessed=30_000_000, transcendentals=0
        ),
    )(images, noise_field, stem, level_one, down, level_two, up, out_t, mlp_in)


def mlp_kernel(
    rows,
    cols,
    chunk,
    patches,
    embed_weight,
    embed_bias,
    mlp_in,
    in_swapped,
    mlp_out,
    encoded,
    own_patches,
    row_patches,
    all_patches,
    embed_w,
    w_in,
    w_out,
    w_other,
    statistics,
    values,
    normed,
    partial_out,
    partial_in,
    hidden,
    total,
    pair_out,
    pair_in,
    last_out,
    last_in,
    load_sem,
    gather_send,
    gather_recv,
    spread_send,
    spread_recv,
    share_send,
    share_recv,
    rs_send,
    rs_recv,
    ag_send,
    ag_recv,
    swap_sem,
    pair_send,
    pair_recv,
    last_send,
    last_recv,
):
    row = lax.axis_index("row")
    col = lax.axis_index("col")
    z = col // 2
    core = col % 2
    depth = cols // 2
    last = depth - 1
    sibling = {"col": col + 1 - 2 * core}
    width = w_in.shape[2]
    height = w_out.shape[0]

    loads = [
        pltpu.make_async_copy(embed_weight, embed_w, load_sem.at[0]),
        pltpu.make_async_copy(
            mlp_in.at[:, pl.ds(pl.multiple_of(core * width, 128), width)],
            w_in.at[core],
            load_sem.at[1],
        ),
        pltpu.make_async_copy(in_swapped, w_in.at[1 - core], load_sem.at[2]),
        pltpu.make_async_copy(
            mlp_out.at[pl.ds(pl.multiple_of(core * height, 16), height), :],
            w_out,
            load_sem.at[3],
        ),
    ]
    for load in loads:
        load.start()
    own_patches[...] = patches[...]

    barrier = pltpu.get_barrier_semaphore()
    for step in range(1, cols):
        pl.semaphore_signal(
            barrier, inc=1, device_id={"col": (col + step) % cols}, device_id_type=MESH
        )
    for step in range(1, rows):
        pl.semaphore_signal(
            barrier, inc=1, device_id={"row": (row + step) % rows}, device_id_type=MESH
        )
    pl.semaphore_wait(barrier, cols - 1 + rows - 1)

    gathers = [
        remote(
            own_patches,
            row_patches.at[col],
            gather_send.at[step],
            gather_recv.at[step],
            {"col": (col + step) % cols},
        )
        for step in range(1, cols)
    ]
    for gather in gathers:
        gather.start()
    row_patches[col] = own_patches[...]
    for gather in gathers:
        gather.wait_recv()
    per_row = row_patches.shape[0] * row_patches.shape[1]
    all_patches[row] = row_patches[...].reshape(per_row, row_patches.shape[2]).astype(bf16)
    spreads = [
        remote(
            all_patches.at[row],
            all_patches.at[row],
            spread_send.at[step],
            spread_recv.at[step],
            {"row": (row + step) % rows},
        )
        for step in range(1, rows)
    ]
    for spread in spreads:
        spread.start()
    tokens = rows * per_row
    part_rows = per_row // 2
    pixels = embed_w.shape[0]
    features = embed_w.shape[1]
    span = features // cols
    loads[0].wait()

    def embed(tokens_in, at):
        at = pl.multiple_of(at, 128)
        return (
            (dot(tokens_in, embed_w[:, pl.ds(at, span)]) + embed_bias[0:1, pl.ds(at, span)])
            .astype(bf16)
            .astype(f32)
        )

    row_tokens = all_patches[row][:, 0:pixels]

    def add_statistics(step, sums):
        part = embed(row_tokens, step * span)
        return (
            sums[0] + jnp.sum(part, axis=1, keepdims=True),
            sums[1] + jnp.sum(part * part, axis=1, keepdims=True),
        )

    zeros = jnp.zeros((per_row, 1), f32)
    value_sums, square_sums = lax.fori_loop(0, cols, add_statistics, (zeros, zeros))
    mean = value_sums / features
    scale = lax.rsqrt(square_sums / features - mean * mean + ln_epsilon)
    lane = lax.broadcasted_iota(jnp.int32, (per_row, 128), 1)
    statistics[row] = jnp.where(lane < 64, mean, scale)
    shares = [
        remote(
            statistics.at[row],
            statistics.at[row],
            share_send.at[step],
            share_recv.at[step],
            {"row": (row + step) % rows},
        )
        for step in range(1, rows)
    ]
    for share in shares:
        share.start()
    for spread in spreads:
        spread.wait_recv()
    swap = remote(
        mlp_out.at[pl.ds(pl.multiple_of((1 - core) * height, 16), height), :],
        w_other,
        swap_sem.at[0],
        swap_sem.at[1],
        sibling,
    )
    swap.start()

    all_tokens = all_patches[...].reshape(tokens, all_patches.shape[2])[:, 0:pixels]
    for j in range(2):
        values[j] = embed(all_tokens, (2 * z + j) * span)
    for share in shares:
        share.wait_recv()
    for half in range(2):
        rows_in = pl.ds(half * part_rows, part_rows)
        known = statistics[:, rows_in, :].reshape(tokens // 2, 128)
        for j in range(2):
            part = values[j].reshape(rows, per_row, span)[
                :, half * part_rows : (half + 1) * part_rows
            ].reshape(tokens // 2, span)
            normed[j, half] = ((part - known[:, 0:1]) * known[:, 64:65]).astype(bf16)
            total[j, half] = jnp.zeros((tokens // 2, span), f32)
    loads[1].wait()
    loads[2].wait()

    chunks = partial_out.shape[1]
    per_half = chunks // 2
    place = (z, last - z)
    ahead = ({"col": col + 2}, {"col": col - 2})
    behind = ({"col": col - 2}, {"col": col + 2})

    def rs_copy(d, i):
        return remote(
            partial_out.at[d, i], partial_in.at[d, i], rs_send.at[d, i], rs_recv.at[d, i], ahead[d]
        )

    def ag_copy(d, i):
        return remote(
            hidden.at[d, i], hidden.at[d, i], ag_send.at[d, i], ag_recv.at[d, i], behind[d]
        )

    def pair_copy(half):
        return remote(
            pair_out.at[half],
            pair_in.at[half],
            pair_send.at[half],
            pair_recv.at[half],
            sibling,
        )

    def final_copies(half):
        return [
            remote(
                last_out.at[half, (row + step) % rows],
                last_in.at[half, step],
                last_send.at[half, step],
                last_recv.at[half, step],
                {"row": (row + step) % rows},
            )
            for step in range(1, rows)
        ]

    def pair_up(half):
        pair_out[half] = total[1, half].astype(bf16)
        pair_copy(half).start()

    def send_final(half):
        pair_copy(half).wait_recv()
        summed = total[0, half] + pair_in[half].astype(f32)
        last_out[half] = summed.astype(bf16).reshape(rows, part_rows, span)
        for final in final_copies(half):
            final.start()

    def finish(half):
        at = pl.ds(pl.multiple_of(row * per_row + half * part_rows, 16), part_rows)
        result = values[core, at, :] + last_out[half, row].astype(f32)
        for step, final in enumerate(final_copies(half)):
            final.wait_recv()
            result = result + last_in[half, step + 1].astype(f32)
        encoded[half * part_rows : (half + 1) * part_rows, :] = result.astype(bf16)

    first_done = per_half - 1 + LAG * (2 * last - jnp.minimum(place[0], place[1]))

    def slot(t, carry):
        @pl.when(t == LAG * last)
        def _():
            loads[3].wait()
            swap.wait_recv()

        for d in range(2):
            i = t - LAG * (2 * last - place[d])

            @pl.when((i >= 0) & (i < chunks) & (place[d] < last))
            def _():
                ag_copy(d, i).wait_recv()

                @pl.when(place[d] > 0)
                def _():
                    ag_copy(d, i).start()

        for d in range(2):
            i = t - LAG * place[d]

            @pl.when((i >= 0) & (i < chunks))
            def _():
                half = i // per_half
                at = pl.multiple_of((d * per_half + i % per_half) * chunk, chunk)
                mine = dot(normed[0, half], w_in[0, :, pl.ds(at, chunk)]) + dot(
                    normed[1, half], w_in[1, :, pl.ds(at, chunk)]
                )

                @pl.when(place[d] == 0)
                def _():
                    partial_out[d, i] = mine.astype(bf16)

                @pl.when(place[d] > 0)
                def _():
                    rs_copy(d, i).wait_recv()
                    whole = mine + partial_in[d, i].astype(f32)

                    @pl.when(place[d] < last)
                    def _():
                        partial_out[d, i] = whole.astype(bf16)

                    @pl.when(place[d] == last)
                    def _():
                        hidden[d, i] = jax.nn.gelu(whole).astype(bf16)

                @pl.when(place[d] < last)
                def _():
                    rs_copy(d, i).start()

                @pl.when(place[d] == last)
                def _():
                    ag_copy(d, i).start()

        for d in range(2):
            i = t - LAG * (2 * last - place[d])

            @pl.when((i >= 0) & (i < chunks))
            def _():
                half = i // per_half
                at = pl.multiple_of((d * per_half + i % per_half) * chunk, chunk)
                total[0, half] += dot(hidden[d, i], w_out[pl.ds(at, chunk), :])
                total[1, half] += dot(hidden[d, i], w_other[pl.ds(at, chunk), :])

        @pl.when(t == first_done)
        def _():
            pair_up(0)

        @pl.when(t == first_done + 2)
        def _():
            send_final(0)

        return carry

    lax.fori_loop(0, chunks + 2 * LAG * last, slot, 0)

    pair_up(1)
    finish(0)
    send_final(1)
    finish(1)

    finals = [final for half in range(2) for final in final_copies(half)]
    pairs = [pair_copy(half) for half in range(2)]
    for copy in gathers + spreads + shares + finals + pairs + [swap]:
        copy.wait_send()

    def drain(i, carry):
        for d in range(2):

            @pl.when(place[d] < last)
            def _():
                rs_copy(d, i).wait_send()

            @pl.when(place[d] > 0)
            def _():
                ag_copy(d, i).wait_send()

        return carry

    lax.fori_loop(0, chunks, drain, 0)


def run_mlp(
    rows, cols, patches, embed_weight, embed_bias, mlp_in, in_swapped, mlp_out
):
    per_device, pixels = patches.shape
    per_row = cols * per_device
    tokens = rows * per_row
    features = embed_weight.shape[1]
    span = features // cols
    width = in_swapped.shape[1]
    chunk = min(256, width // 2)
    chunks = 2 * (width // 2 // chunk)
    half = tokens // 2
    vmem = pl.BlockSpec(memory_space=pltpu.VMEM)
    anywhere = pl.BlockSpec(memory_space=pl.ANY)
    dma = pltpu.SemaphoreType.DMA
    return pl.pallas_call(
        functools.partial(mlp_kernel, rows, cols, chunk),
        out_shape=jax.ShapeDtypeStruct((per_row, span), bf16),
        in_specs=[vmem, anywhere, vmem, anywhere, anywhere, anywhere],
        out_specs=vmem,
        scratch_shapes=[
            pltpu.VMEM((per_device, pixels), f32),
            pltpu.VMEM((cols, per_device, pixels), f32),
            pltpu.VMEM((rows, per_row, pixels), bf16),
            pltpu.VMEM(embed_weight.shape, bf16),
            pltpu.VMEM((2,) + in_swapped.shape, bf16),
            pltpu.VMEM((width, span), bf16),
            pltpu.VMEM((width, span), bf16),
            pltpu.VMEM((rows, per_row, 128), f32),
            pltpu.VMEM((2, tokens, span), f32),
            pltpu.VMEM((2, 2, half, span), bf16),
            pltpu.VMEM((2, chunks, half, chunk), bf16),
            pltpu.VMEM((2, chunks, half, chunk), bf16),
            pltpu.VMEM((2, chunks, half, chunk), bf16),
            pltpu.VMEM((2, 2, half, span), f32),
            pltpu.VMEM((2, half, span), bf16),
            pltpu.VMEM((2, half, span), bf16),
            pltpu.VMEM((2, rows, per_row // 2, span), bf16),
            pltpu.VMEM((2, rows, per_row // 2, span), bf16),
            dma((4,)),
            dma((cols,)),
            dma((cols,)),
            dma((rows,)),
            dma((rows,)),
            dma((rows,)),
            dma((rows,)),
            dma((2, chunks)),
            dma((2, chunks)),
            dma((2, chunks)),
            dma((2, chunks)),
            dma((2,)),
            dma((2,)),
            dma((2,)),
            dma((2, rows)),
            dma((2, rows)),
        ],
        compiler_params=pltpu.CompilerParams(
            collective_id=1, has_side_effects=True, vmem_limit_bytes=56 * MIB
        ),
        cost_estimate=pl.CostEstimate(
            flops=10_000_000_000, bytes_accessed=30_000_000, transcendentals=0
        ),
    )(patches, embed_weight, embed_bias, mlp_in, in_swapped, mlp_out)


def on_device(
    images,
    noise_field,
    stem_weight,
    level_one,
    down_weight,
    level_two,
    up_weight,
    out_weight,
    embed_weight,
    embed_bias,
    mlp_in,
    mlp_out,
):
    rows = lax.axis_size("row")
    cols = lax.axis_size("col")
    lines, in_swapped = run_score(
        images.transpose(1, 3, 0, 2),
        noise_field.transpose(1, 3, 0, 2),
        stem_weight,
        level_one,
        down_weight,
        level_two,
        up_weight,
        out_weight.T,
        mlp_in,
    )
    count = images.shape[0]
    purified = lines.transpose(2, 0, 3, 1)
    grid = SIDE // PATCH
    patches = lines.astype(bf16).reshape(grid, PATCH, 3, count, grid, PATCH)
    patches = patches.transpose(3, 0, 4, 1, 5, 2).reshape(count * grid * grid, PATCH * PATCH * 3)
    pixels = patches.shape[1]
    patches = jnp.pad(patches.astype(f32), ((0, 0), (0, -pixels % 128)))
    encoded = run_mlp(
        rows,
        cols,
        patches,
        embed_weight,
        embed_bias[None, :],
        mlp_in,
        in_swapped,
        mlp_out,
    )
    return (purified, encoded)


def solution(mesh):
    placed = (
        P(("row", "col"), None, None, None),
        P(("row", "col"), None, None, None),
        P(),
        P(),
        P(),
        P(),
        P(),
        P(),
        P(),
        P(),
        P("col", "row"),
        P("row", "col"),
    )
    return jax.shard_map(
        on_device,
        mesh=mesh,
        in_specs=placed,
        out_specs=(P(("row", "col"), None, None, None), P("row", "col")),
        check_vma=False,
    )
```

```python
import functools
import math

import jax
import jax.numpy as jnp
from jax import lax
from jax.experimental import pallas as pl
from jax.experimental.pallas import tpu as pltpu
from jax.sharding import PartitionSpec as P

PATCH = 14
SIDE = 28
WIDE = 32
HALF = 14
HWIDE = 16

step_size = 0.25
noise_gain = math.sqrt(0.5)
ln_epsilon = 1e-06
LAG = 2
MESH = pl.DeviceIdType.MESH
MIB = 1024 * 1024
f32 = jnp.float32
bf16 = jnp.bfloat16


def dot(a, b):
    return jnp.dot(a, b, preferred_element_type=f32)


def remote(src, dst, send_sem, recv_sem, device):
    return pltpu.make_async_remote_copy(
        src_ref=src,
        dst_ref=dst,
        send_sem=send_sem,
        recv_sem=recv_sem,
        device_id=device,
        device_id_type=MESH,
    )


def masked_act(stream, wide, side):
    column = lax.broadcasted_iota(jnp.int32, stream.shape, 0) & (wide - 1)
    return jnp.where(column < side, jax.nn.gelu(stream), 0.0)


def put_act(field, at, stream, wide, side):
    depth = stream.shape[1]
    rows = stream.shape[0]
    act = masked_act(stream, wide, side)
    field[pl.ds(at, rows), 0:depth] = pltpu.roll(act, 1, 0).astype(bf16)
    field[pl.ds(at, rows), depth : 2 * depth] = act.astype(bf16)
    field[pl.ds(at, rows), 2 * depth : 3 * depth] = pltpu.roll(act, rows - 1, 0).astype(bf16)


def conv_rows(field, weight, at, rows, wide):
    around = [
        field[at + row_off * wide : at + row_off * wide + rows, :] for row_off in range(3)
    ]
    return dot(jnp.concatenate(around, axis=1), weight[...])


def score_kernel(
    images,
    noise_field,
    stem_weight,
    level_one_hbm,
    down_hbm,
    level_two_hbm,
    up_hbm,
    out_t,
    mlp_in,
    purified,
    in_swapped,
    pixels,
    noise,
    result,
    stem,
    level_one,
    down,
    level_two,
    up,
    field_a,
    field_b,
    coarse_a,
    coarse_b,
    stream,
    halves,
    coarse,
    load_sem,
    swap_sem,
):
    loads = [
        pltpu.make_async_copy(level_one_hbm.at[k], level_one.at[k], load_sem.at[k])
        for k in range(4)
    ]
    loads.append(pltpu.make_async_copy(down_hbm, down, load_sem.at[4]))
    loads.append(pltpu.make_async_copy(level_two_hbm, level_two, load_sem.at[5]))
    loads.append(pltpu.make_async_copy(up_hbm, up, load_sem.at[6]))
    for k in (0, 1, 4, 5, 6, 2, 3):
        loads[k].start()
    col = lax.axis_index("col")
    core = col % 2
    sibling = {"col": col + 1 - 2 * core}
    barrier = pltpu.get_barrier_semaphore()
    pl.semaphore_signal(barrier, inc=1, device_id=sibling, device_id_type=MESH)
    pl.semaphore_wait(barrier, 1)
    width = mlp_in.shape[1] // 2
    swap = remote(
        mlp_in.at[:, pl.ds(pl.multiple_of((1 - core) * width, 128), width)],
        in_swapped,
        swap_sem.at[0],
        swap_sem.at[1],
        sibling,
    )
    swap.start()

    depth = stream.shape[1]
    count = pixels.shape[0]
    for planes, given in ((pixels, images), (noise, noise_field)):
        planes[...] = jnp.zeros(planes.shape, f32)
        for n in range(count):
            for y in range(SIDE):
                planes[n, 0:3, y * WIDE : y * WIDE + SIDE] = given[y, :, n, :]
    stem[...] = jnp.zeros(stem.shape, f32)
    stem_rows = stem_weight[...].astype(f32)
    for g in range(9):
        stem[8 * g : 8 * g + 3, :] = stem_rows[3 * g : 3 * g + 3, :]
    cells = SIDE * WIDE
    ccells = HALF * HWIDE
    tile = HALF * WIDE
    for field, row, last in (
        (field_a, WIDE, cells),
        (field_b, WIDE, cells),
        (coarse_a, HWIDE, ccells),
        (coarse_b, HWIDE, ccells),
    ):
        field[0:row, :] = jnp.zeros((row, 3 * depth), bf16)
        field[row + last : row + last + row, :] = jnp.zeros((row, 3 * depth), bf16)

    def one_image(n, carry):
        def arrived(*which):
            @pl.when(n == 0)
            def _():
                for k in which:
                    loads[k].wait()

        view = pixels[n].astype(bf16).astype(f32)
        lanes = view.shape[1]
        groups = []
        for row_off in (-1, 0, 1):
            for col_off in (-1, 0, 1):
                shift = (-(row_off * WIDE + col_off)) % lanes
                groups.append(pltpu.roll(view, shift, 1) if shift else view)
        groups.extend([jnp.zeros_like(view)] * 7)
        columns = jnp.concatenate(groups, axis=0).T.astype(bf16)
        for at in range(0, cells, tile):
            now = dot(columns[at : at + tile, :], stem[...].astype(bf16))
            stream[at : at + tile, :] = now
            put_act(field_a, WIDE + at, now, WIDE, SIDE)
        arrived(0)
        for at in range(0, cells, tile):
            now = stream[at : at + tile, :] + conv_rows(
                field_a, level_one.at[0], at, tile, WIDE
            )
            stream[at : at + tile, :] = now
            put_act(field_b, WIDE + at, now, WIDE, SIDE)
        arrived(1)
        for at in range(0, cells, tile):
            now = stream[at : at + tile, :] + conv_rows(
                field_b, level_one.at[1], at, tile, WIDE
            )
            stream[at : at + tile, :] = now
            for h in range(depth // 128):
                stream_halves[h][at : at + tile, :] = now[:, h * 128 : (h + 1) * 128]
        arrived(4, 5, 6)
        now = None
        for b in range(2):
            parts = [
                half[pl.ds(b, cells // 2, stride=2), :].astype(bf16).reshape(HALF, 2, HWIDE, 128)
                for half in stream_halves
            ]
            for a in range(2):
                piece = jnp.concatenate(
                    [part[:, a].reshape(ccells, 128) for part in parts], axis=1
                )
                at = (2 * a + b) * depth
                part = dot(piece, down[at : at + depth, :])
                now = part if now is None else now + part
        put_act(coarse_a, HWIDE, now, HWIDE, HALF)
        now = now + conv_rows(coarse_a, level_two.at[0], 0, ccells, HWIDE)
        put_act(coarse_b, HWIDE, now, HWIDE, HALF)
        now = now + conv_rows(coarse_b, level_two.at[1], 0, ccells, HWIDE)
        lifted = now.astype(bf16)
        for b in range(2):
            pieces = [
                dot(lifted, up[:, (2 * a + b) * depth : (2 * a + b + 1) * depth]).reshape(
                    HALF, 1, HWIDE, depth
                )
                for a in range(2)
            ]
            both = jnp.concatenate(pieces, axis=1).reshape(cells // 2, depth)
            for h in range(depth // 128):
                stream_halves[h][pl.ds(b, cells // 2, stride=2), :] = both[
                    :, h * 128 : (h + 1) * 128
                ]
        for at in range(0, cells, tile):
            now = stream[at : at + tile, :] + jnp.concatenate(
                [half[at : at + tile, :] for half in stream_halves], axis=1
            )
            stream[at : at + tile, :] = now
            put_act(field_a, WIDE + at, now, WIDE, SIDE)
        arrived(2, 3)
        for at in range(0, cells, tile):
            now = stream[at : at + tile, :] + conv_rows(
                field_a, level_one.at[2], at, tile, WIDE
            )
            stream[at : at + tile, :] = now
            put_act(field_b, WIDE + at, now, WIDE, SIDE)
        for at in range(0, cells, tile):
            now = stream[at : at + tile, :] + conv_rows(
                field_b, level_one.at[3], at, tile, WIDE
            )
            coarse[at : at + tile, :] = jax.nn.gelu(now).astype(bf16)
        score = lax.dot_general(
            out_t[...], coarse[...], (((1,), (1,)), ((), ())), preferred_element_type=f32
        )
        result[n, 0:3, :] = (
            pixels[n, 0:3, :] + step_size * score + noise_gain * noise[n, 0:3, :]
        )
        return carry

    stream_halves = [halves.at[h] for h in range(depth // 128)]
    coarse[cells:, :] = jnp.zeros((coarse.shape[0] - cells, depth), bf16)
    lax.fori_loop(0, count, one_image, 0)
    for n in range(count):
        for y in range(SIDE):
            purified[y, :, n, :] = result[n, 0:3, y * WIDE : y * WIDE + SIDE]
    swap.wait()


def run_score(images, noise_field, stem, level_one, down, level_two, up, out_t, mlp_in):
    depth = stem.shape[1]
    vmem = pl.BlockSpec(memory_space=pltpu.VMEM)
    anywhere = pl.BlockSpec(memory_space=pl.ANY)
    return pl.pallas_call(
        score_kernel,
        out_shape=(
            jax.ShapeDtypeStruct(images.shape, f32),
            jax.ShapeDtypeStruct((mlp_in.shape[0], mlp_in.shape[1] // 2), bf16),
        ),
        in_specs=[vmem] * 3 + [anywhere] * 4 + [vmem, anywhere],
        out_specs=(vmem, anywhere),
        scratch_shapes=[
            pltpu.VMEM((images.shape[2], 8, WIDE * WIDE), f32),
            pltpu.VMEM((images.shape[2], 8, WIDE * WIDE), f32),
            pltpu.VMEM((images.shape[2], 8, WIDE * WIDE), f32),
            pltpu.VMEM((128, depth), f32),
            pltpu.VMEM(level_one.shape, bf16),
            pltpu.VMEM(down.shape, bf16),
            pltpu.VMEM(level_two.shape, bf16),
            pltpu.VMEM(up.shape, bf16),
            pltpu.VMEM(((SIDE + 2) * WIDE, 3 * depth), bf16),
            pltpu.VMEM(((SIDE + 2) * WIDE, 3 * depth), bf16),
            pltpu.VMEM(((HALF + 2) * HWIDE, 3 * depth), bf16),
            pltpu.VMEM(((HALF + 2) * HWIDE, 3 * depth), bf16),
            pltpu.VMEM((SIDE * WIDE, depth), f32),
            pltpu.VMEM((depth // 128, SIDE * WIDE, 128), f32),
            pltpu.VMEM((WIDE * WIDE, depth), bf16),
            pltpu.SemaphoreType.DMA((7,)),
            pltpu.SemaphoreType.DMA((2,)),
        ],
        compiler_params=pltpu.CompilerParams(
            collective_id=0, has_side_effects=True, vmem_limit_bytes=60 * MIB
        ),
        cost_estimate=pl.CostEstimate(
            flops=10_000_000_000, bytes_accessed=30_000_000, transcendentals=0
        ),
    )(images, noise_field, stem, level_one, down, level_two, up, out_t, mlp_in)


def mlp_kernel(
    rows,
    cols,
    chunk,
    patches,
    embed_weight,
    embed_bias,
    mlp_in,
    in_swapped,
    mlp_out,
    encoded,
    own_patches,
    row_patches,
    all_patches,
    embed_w,
    w_in,
    w_out,
    w_other,
    statistics,
    values,
    normed,
    mine,
    partial_out,
    partial_in,
    hidden,
    total,
    pair_out,
    pair_in,
    last_out,
    last_in,
    load_sem,
    gather_send,
    gather_recv,
    spread_send,
    spread_recv,
    share_send,
    share_recv,
    rs_send,
    rs_recv,
    ag_send,
    ag_recv,
    swap_sem,
    pair_send,
    pair_recv,
    last_send,
    last_recv,
):
    row = lax.axis_index("row")
    col = lax.axis_index("col")
    z = col // 2
    core = col % 2
    depth = cols // 2
    last = depth - 1
    sibling = {"col": col + 1 - 2 * core}
    width = w_in.shape[2]
    height = w_out.shape[0]

    loads = [
        pltpu.make_async_copy(embed_weight, embed_w, load_sem.at[0]),
        pltpu.make_async_copy(
            mlp_in.at[:, pl.ds(pl.multiple_of(core * width, 128), width)],
            w_in.at[core],
            load_sem.at[1],
        ),
        pltpu.make_async_copy(in_swapped, w_in.at[1 - core], load_sem.at[2]),
        pltpu.make_async_copy(
            mlp_out.at[pl.ds(pl.multiple_of(core * height, 16), height), :],
            w_out,
            load_sem.at[3],
        ),
    ]
    for load in loads:
        load.start()
    own_patches[...] = patches[...]

    barrier = pltpu.get_barrier_semaphore()
    for step in range(1, cols):
        pl.semaphore_signal(
            barrier, inc=1, device_id={"col": (col + step) % cols}, device_id_type=MESH
        )
    for step in range(1, rows):
        pl.semaphore_signal(
            barrier, inc=1, device_id={"row": (row + step) % rows}, device_id_type=MESH
        )
    pl.semaphore_wait(barrier, cols - 1 + rows - 1)

    gathers = [
        remote(
            own_patches,
            row_patches.at[col],
            gather_send.at[step],
            gather_recv.at[step],
            {"col": (col + step) % cols},
        )
        for step in range(1, cols)
    ]
    for gather in gathers:
        gather.start()
    row_patches[col] = own_patches[...]
    for gather in gathers:
        gather.wait_recv()
    per_row = row_patches.shape[0] * row_patches.shape[1]
    all_patches[row] = row_patches[...].reshape(per_row, row_patches.shape[2]).astype(bf16)
    spreads = [
        remote(
            all_patches.at[row],
            all_patches.at[row],
            spread_send.at[step],
            spread_recv.at[step],
            {"row": (row + step) % rows},
        )
        for step in range(1, rows)
    ]
    for spread in spreads:
        spread.start()
    tokens = rows * per_row
    part_rows = per_row // 2
    pixels = embed_w.shape[0]
    features = embed_w.shape[1]
    span = features // cols
    loads[0].wait()

    def embed(tokens_in, at):
        at = pl.multiple_of(at, 128)
        return (
            (dot(tokens_in, embed_w[:, pl.ds(at, span)]) + embed_bias[0:1, pl.ds(at, span)])
            .astype(bf16)
            .astype(f32)
        )

    row_tokens = all_patches[row][:, 0:pixels]

    def add_statistics(step, sums):
        part = embed(row_tokens, step * span)
        return (
            sums[0] + jnp.sum(part, axis=1, keepdims=True),
            sums[1] + jnp.sum(part * part, axis=1, keepdims=True),
        )

    zeros = jnp.zeros((per_row, 1), f32)
    value_sums, square_sums = lax.fori_loop(0, cols, add_statistics, (zeros, zeros))
    mean = value_sums / features
    scale = lax.rsqrt(square_sums / features - mean * mean + ln_epsilon)
    lane = lax.broadcasted_iota(jnp.int32, (per_row, 128), 1)
    statistics[row] = jnp.where(lane < 64, mean, scale)
    shares = [
        remote(
            statistics.at[row],
            statistics.at[row],
            share_send.at[step],
            share_recv.at[step],
            {"row": (row + step) % rows},
        )
        for step in range(1, rows)
    ]
    for share in shares:
        share.start()
    for spread in spreads:
        spread.wait_recv()
    swap = remote(
        mlp_out.at[pl.ds(pl.multiple_of((1 - core) * height, 16), height), :],
        w_other,
        swap_sem.at[0],
        swap_sem.at[1],
        sibling,
    )
    swap.start()

    all_tokens = all_patches[...].reshape(tokens, all_patches.shape[2])[:, 0:pixels]
    for j in range(2):
        values[j] = embed(all_tokens, (2 * z + j) * span)
    for share in shares:
        share.wait_recv()
    for half in range(2):
        rows_in = pl.ds(half * part_rows, part_rows)
        known = statistics[:, rows_in, :].reshape(tokens // 2, 128)
        for j in range(2):
            part = values[j].reshape(rows, per_row, span)[
                :, half * part_rows : (half + 1) * part_rows
            ].reshape(tokens // 2, span)
            normed[j, half] = ((part - known[:, 0:1]) * known[:, 64:65]).astype(bf16)
            total[j, half] = jnp.zeros((tokens // 2, span), f32)
    loads[1].wait()
    loads[2].wait()

    chunks = partial_out.shape[1]
    per_half = chunks // 2
    place = (z, last - z)
    ahead = ({"col": col + 2}, {"col": col - 2})
    behind = ({"col": col - 2}, {"col": col + 2})

    def rs_copy(d, i):
        return remote(
            partial_out.at[d, i], partial_in.at[d, i], rs_send.at[d, i], rs_recv.at[d, i], ahead[d]
        )

    def ag_copy(d, i):
        return remote(
            hidden.at[d, i], hidden.at[d, i], ag_send.at[d, i], ag_recv.at[d, i], behind[d]
        )

    def pair_copy(half):
        return remote(
            pair_out.at[half],
            pair_in.at[half],
            pair_send.at[half],
            pair_recv.at[half],
            sibling,
        )

    def final_copies(half):
        return [
            remote(
                last_out.at[half, (row + step) % rows],
                last_in.at[half, step],
                last_send.at[half, step],
                last_recv.at[half, step],
                {"row": (row + step) % rows},
            )
            for step in range(1, rows)
        ]

    def pair_up(half):
        pair_out[half] = total[1, half].astype(bf16)
        pair_copy(half).start()

    def send_final(half):
        pair_copy(half).wait_recv()
        summed = total[0, half] + pair_in[half].astype(f32)
        last_out[half] = summed.astype(bf16).reshape(rows, part_rows, span)
        for final in final_copies(half):
            final.start()

    def finish(half):
        at = pl.ds(pl.multiple_of(row * per_row + half * part_rows, 16), part_rows)
        result = values[core, at, :] + last_out[half, row].astype(f32)
        for step, final in enumerate(final_copies(half)):
            final.wait_recv()
            result = result + last_in[half, step + 1].astype(f32)
        encoded[half * part_rows : (half + 1) * part_rows, :] = result.astype(bf16)

    first_done = per_half - 1 + LAG * (2 * last - jnp.minimum(place[0], place[1]))

    def slot(t, carry):
        @pl.when(t == LAG * last)
        def _():
            loads[3].wait()
            swap.wait_recv()

        for d in range(2):
            i = t - LAG * (2 * last - place[d])

            @pl.when((i >= 0) & (i < chunks) & (place[d] < last))
            def _():
                ag_copy(d, i).wait_recv()

                @pl.when(place[d] > 0)
                def _():
                    ag_copy(d, i).start()

        for d in range(2):
            i = t - LAG * place[d]

            @pl.when((i >= 0) & (i < chunks))
            def _():
                half = i // per_half
                at = pl.multiple_of((d * per_half + i % per_half) * chunk, chunk)

                @pl.when(half == 0)
                def _():
                    both = dot(
                        normed[0].reshape(tokens, span), w_in[0, :, pl.ds(at, chunk)]
                    ) + dot(normed[1].reshape(tokens, span), w_in[1, :, pl.ds(at, chunk)])
                    mine[d, i] = both[0 : tokens // 2]
                    mine[d, i + per_half] = both[tokens // 2 :]

                @pl.when(place[d] == 0)
                def _():
                    partial_out[d, i] = mine[d, i].astype(bf16)

                @pl.when(place[d] > 0)
                def _():
                    rs_copy(d, i).wait_recv()
                    whole = mine[d, i] + partial_in[d, i].astype(f32)

                    @pl.when(place[d] < last)
                    def _():
                        partial_out[d, i] = whole.astype(bf16)

                    @pl.when(place[d] == last)
                    def _():
                        hidden[d, i] = jax.nn.gelu(whole).astype(bf16)

                @pl.when(place[d] < last)
                def _():
                    rs_copy(d, i).start()

                @pl.when(place[d] == last)
                def _():
                    ag_copy(d, i).start()

        for d in range(2):
            i = t - LAG * (2 * last - place[d])

            @pl.when((i >= 0) & (i < chunks))
            def _():
                half = i // per_half
                at = pl.multiple_of((d * per_half + i % per_half) * chunk, chunk)
                total[0, half] += dot(hidden[d, i], w_out[pl.ds(at, chunk), :])
                total[1, half] += dot(hidden[d, i], w_other[pl.ds(at, chunk), :])

        @pl.when(t == first_done)
        def _():
            pair_up(0)

        @pl.when(t == first_done + 2)
        def _():
            send_final(0)

        return carry

    lax.fori_loop(0, chunks + 2 * LAG * last, slot, 0)

    pair_up(1)
    finish(0)
    send_final(1)
    finish(1)

    finals = [final for half in range(2) for final in final_copies(half)]
    pairs = [pair_copy(half) for half in range(2)]
    for copy in gathers + spreads + shares + finals + pairs + [swap]:
        copy.wait_send()

    def drain(i, carry):
        for d in range(2):

            @pl.when(place[d] < last)
            def _():
                rs_copy(d, i).wait_send()

            @pl.when(place[d] > 0)
            def _():
                ag_copy(d, i).wait_send()

        return carry

    lax.fori_loop(0, chunks, drain, 0)


def run_mlp(
    rows, cols, patches, embed_weight, embed_bias, mlp_in, in_swapped, mlp_out
):
    per_device, pixels = patches.shape
    per_row = cols * per_device
    tokens = rows * per_row
    features = embed_weight.shape[1]
    span = features // cols
    width = in_swapped.shape[1]
    chunk = min(256, width // 2)
    chunks = 2 * (width // 2 // chunk)
    half = tokens // 2
    vmem = pl.BlockSpec(memory_space=pltpu.VMEM)
    anywhere = pl.BlockSpec(memory_space=pl.ANY)
    dma = pltpu.SemaphoreType.DMA
    return pl.pallas_call(
        functools.partial(mlp_kernel, rows, cols, chunk),
        out_shape=jax.ShapeDtypeStruct((per_row, span), bf16),
        in_specs=[vmem, anywhere, vmem, anywhere, anywhere, anywhere],
        out_specs=vmem,
        scratch_shapes=[
            pltpu.VMEM((per_device, pixels), f32),
            pltpu.VMEM((cols, per_device, pixels), f32),
            pltpu.VMEM((rows, per_row, pixels), bf16),
            pltpu.VMEM(embed_weight.shape, bf16),
            pltpu.VMEM((2,) + in_swapped.shape, bf16),
            pltpu.VMEM((width, span), bf16),
            pltpu.VMEM((width, span), bf16),
            pltpu.VMEM((rows, per_row, 128), f32),
            pltpu.VMEM((2, tokens, span), f32),
            pltpu.VMEM((2, 2, half, span), bf16),
            pltpu.VMEM((2, chunks, half, chunk), f32),
            pltpu.VMEM((2, chunks, half, chunk), bf16),
            pltpu.VMEM((2, chunks, half, chunk), bf16),
            pltpu.VMEM((2, chunks, half, chunk), bf16),
            pltpu.VMEM((2, 2, half, span), f32),
            pltpu.VMEM((2, half, span), bf16),
            pltpu.VMEM((2, half, span), bf16),
            pltpu.VMEM((2, rows, per_row // 2, span), bf16),
            pltpu.VMEM((2, rows, per_row // 2, span), bf16),
            dma((4,)),
            dma((cols,)),
            dma((cols,)),
            dma((rows,)),
            dma((rows,)),
            dma((rows,)),
            dma((rows,)),
            dma((2, chunks)),
            dma((2, chunks)),
            dma((2, chunks)),
            dma((2, chunks)),
            dma((2,)),
            dma((2,)),
            dma((2,)),
            dma((2, rows)),
            dma((2, rows)),
        ],
        compiler_params=pltpu.CompilerParams(
            collective_id=1, has_side_effects=True, vmem_limit_bytes=56 * MIB
        ),
        cost_estimate=pl.CostEstimate(
            flops=10_000_000_000, bytes_accessed=30_000_000, transcendentals=0
        ),
    )(patches, embed_weight, embed_bias, mlp_in, in_swapped, mlp_out)


def on_device(
    images,
    noise_field,
    stem_weight,
    level_one,
    down_weight,
    level_two,
    up_weight,
    out_weight,
    embed_weight,
    embed_bias,
    mlp_in,
    mlp_out,
):
    rows = lax.axis_size("row")
    cols = lax.axis_size("col")
    lines, in_swapped = run_score(
        images.transpose(1, 3, 0, 2),
        noise_field.transpose(1, 3, 0, 2),
        stem_weight,
        level_one,
        down_weight,
        level_two,
        up_weight,
        out_weight.T,
        mlp_in,
    )
    count = images.shape[0]
    purified = lines.transpose(2, 0, 3, 1)
    grid = SIDE // PATCH
    patches = lines.astype(bf16).reshape(grid, PATCH, 3, count, grid, PATCH)
    patches = patches.transpose(3, 0, 4, 1, 5, 2).reshape(count * grid * grid, PATCH * PATCH * 3)
    pixels = patches.shape[1]
    patches = jnp.pad(patches.astype(f32), ((0, 0), (0, -pixels % 128)))
    encoded = run_mlp(
        rows,
        cols,
        patches,
        embed_weight,
        embed_bias[None, :],
        mlp_in,
        in_swapped,
        mlp_out,
    )
    return (purified, encoded)


def solution(mesh):
    placed = (
        P(("row", "col"), None, None, None),
        P(("row", "col"), None, None, None),
        P(),
        P(),
        P(),
        P(),
        P(),
        P(),
        P(),
        P(),
        P("col", "row"),
        P("row", "col"),
    )
    return jax.shard_map(
        on_device,
        mesh=mesh,
        in_specs=placed,
        out_specs=(P(("row", "col"), None, None, None), P("row", "col")),
        check_vma=False,
    )
```

```python
import functools
import math

import jax
import jax.numpy as jnp
from jax import lax
from jax.experimental import pallas as pl
from jax.experimental.pallas import tpu as pltpu
from jax.sharding import PartitionSpec as P

PATCH = 14
SIDE = 28
WIDE = 32
HALF = 14
HWIDE = 16

step_size = 0.25
noise_gain = math.sqrt(0.5)
ln_epsilon = 1e-06
LAG = 3
MESH = pl.DeviceIdType.MESH
MIB = 1024 * 1024
f32 = jnp.float32
bf16 = jnp.bfloat16


def dot(a, b):
    return jnp.dot(a, b, preferred_element_type=f32)


def remote(src, dst, send_sem, recv_sem, device):
    return pltpu.make_async_remote_copy(
        src_ref=src,
        dst_ref=dst,
        send_sem=send_sem,
        recv_sem=recv_sem,
        device_id=device,
        device_id_type=MESH,
    )


def masked_act(stream, wide, side):
    column = lax.broadcasted_iota(jnp.int32, stream.shape, 0) % wide
    return jnp.where(column < side, jax.nn.gelu(stream), 0.0)


def put_act(field, at, stream, wide, side):
    depth = stream.shape[1]
    rows = stream.shape[0]
    act = masked_act(stream, wide, side)
    field[pl.ds(at, rows), 0:depth] = pltpu.roll(act, 1, 0).astype(bf16)
    field[pl.ds(at, rows), depth : 2 * depth] = act.astype(bf16)
    field[pl.ds(at, rows), 2 * depth : 3 * depth] = pltpu.roll(act, rows - 1, 0).astype(bf16)


def conv_rows(field, weight, at, rows, wide):
    span = weight.shape[0] // 3
    total = None
    for row_off in range(3):
        part = dot(
            field[at + row_off * wide : at + row_off * wide + rows, :],
            weight[row_off * span : (row_off + 1) * span, :],
        )
        total = part if total is None else total + part
    return total


def score_kernel(
    images,
    noise_field,
    stem_weight,
    level_one_hbm,
    down_hbm,
    level_two_hbm,
    up_hbm,
    out_t,
    mlp_in,
    purified,
    in_swapped,
    pixels,
    noise,
    result,
    stem,
    level_one,
    down,
    level_two,
    up,
    field_a,
    field_b,
    coarse_a,
    coarse_b,
    stream,
    halves,
    coarse,
    load_sem,
    swap_sem,
):
    loads = [
        pltpu.make_async_copy(level_one_hbm.at[k], level_one.at[k], load_sem.at[k])
        for k in range(4)
    ]
    loads.append(pltpu.make_async_copy(down_hbm, down, load_sem.at[4]))
    loads.append(pltpu.make_async_copy(level_two_hbm, level_two, load_sem.at[5]))
    loads.append(pltpu.make_async_copy(up_hbm, up, load_sem.at[6]))
    for k in (0, 1, 4, 5, 6, 2, 3):
        loads[k].start()
    col = lax.axis_index("col")
    core = col % 2
    sibling = {"col": col + 1 - 2 * core}
    barrier = pltpu.get_barrier_semaphore()
    pl.semaphore_signal(barrier, inc=1, device_id=sibling, device_id_type=MESH)
    pl.semaphore_wait(barrier, 1)
    width = mlp_in.shape[1] // 2
    swap = remote(
        mlp_in.at[:, pl.ds(pl.multiple_of((1 - core) * width, 128), width)],
        in_swapped,
        swap_sem.at[0],
        swap_sem.at[1],
        sibling,
    )
    swap.start()

    depth = stream.shape[1]
    count = pixels.shape[0]
    for planes, given in ((pixels, images), (noise, noise_field)):
        planes[...] = jnp.zeros(planes.shape, f32)
        for n in range(count):
            for y in range(SIDE):
                planes[n, 0:3, y * WIDE : y * WIDE + SIDE] = given[y, :, n, :]
    stem[...] = jnp.zeros(stem.shape, f32)
    stem_rows = stem_weight[...].astype(f32)
    for g in range(9):
        stem[8 * g : 8 * g + 3, :] = stem_rows[3 * g : 3 * g + 3, :]
    cells = SIDE * WIDE
    ccells = HALF * HWIDE
    tile = 7 * WIDE
    for field, row, last in (
        (field_a, WIDE, cells),
        (field_b, WIDE, cells),
        (coarse_a, HWIDE, ccells),
        (coarse_b, HWIDE, ccells),
    ):
        field[0:row, :] = jnp.zeros((row, 3 * depth), bf16)
        field[row + last : row + last + row, :] = jnp.zeros((row, 3 * depth), bf16)

    def one_image(n, carry):
        def arrived(*which):
            @pl.when(n == 0)
            def _():
                for k in which:
                    loads[k].wait()

        view = pixels[n].astype(bf16).astype(f32)
        lanes = view.shape[1]
        groups = []
        for row_off in (-1, 0, 1):
            for col_off in (-1, 0, 1):
                shift = (-(row_off * WIDE + col_off)) % lanes
                groups.append(pltpu.roll(view, shift, 1) if shift else view)
        groups.extend([jnp.zeros_like(view)] * 7)
        columns = jnp.concatenate(groups, axis=0).T.astype(bf16)
        for at in range(0, cells, tile):
            now = dot(columns[at : at + tile, :], stem[...].astype(bf16))
            stream[at : at + tile, :] = now
            put_act(field_a, WIDE + at, now, WIDE, SIDE)
        arrived(0)
        for at in range(0, cells, tile):
            now = stream[at : at + tile, :] + conv_rows(
                field_a, level_one.at[0], at, tile, WIDE
            )
            stream[at : at + tile, :] = now
            put_act(field_b, WIDE + at, now, WIDE, SIDE)
        arrived(1)
        for at in range(0, cells, tile):
            now = stream[at : at + tile, :] + conv_rows(
                field_b, level_one.at[1], at, tile, WIDE
            )
            stream[at : at + tile, :] = now
            for h in range(depth // 128):
                stream_halves[h][at : at + tile, :] = now[:, h * 128 : (h + 1) * 128]
        arrived(4, 5, 6)
        now = None
        for b in range(2):
            parts = [
                half[pl.ds(b, cells // 2, stride=2), :].astype(bf16).reshape(HALF, 2, HWIDE, 128)
                for half in stream_halves
            ]
            for a in range(2):
                piece = jnp.concatenate(
                    [part[:, a].reshape(ccells, 128) for part in parts], axis=1
                )
                at = (2 * a + b) * depth
                part = dot(piece, down[at : at + depth, :])
                now = part if now is None else now + part
        put_act(coarse_a, HWIDE, now, HWIDE, HALF)
        now = now + conv_rows(coarse_a, level_two.at[0], 0, ccells, HWIDE)
        put_act(coarse_b, HWIDE, now, HWIDE, HALF)
        now = now + conv_rows(coarse_b, level_two.at[1], 0, ccells, HWIDE)
        lifted = now.astype(bf16)
        for b in range(2):
            pieces = [
                dot(lifted, up[:, (2 * a + b) * depth : (2 * a + b + 1) * depth]).reshape(
                    HALF, 1, HWIDE, depth
                )
                for a in range(2)
            ]
            both = jnp.concatenate(pieces, axis=1).reshape(cells // 2, depth)
            for h in range(depth // 128):
                stream_halves[h][pl.ds(b, cells // 2, stride=2), :] = both[
                    :, h * 128 : (h + 1) * 128
                ]
        for at in range(0, cells, tile):
            now = stream[at : at + tile, :] + jnp.concatenate(
                [half[at : at + tile, :] for half in stream_halves], axis=1
            )
            stream[at : at + tile, :] = now
            put_act(field_a, WIDE + at, now, WIDE, SIDE)
        arrived(2, 3)
        for at in range(0, cells, tile):
            now = stream[at : at + tile, :] + conv_rows(
                field_a, level_one.at[2], at, tile, WIDE
            )
            stream[at : at + tile, :] = now
            put_act(field_b, WIDE + at, now, WIDE, SIDE)
        for at in range(0, cells, tile):
            now = stream[at : at + tile, :] + conv_rows(
                field_b, level_one.at[3], at, tile, WIDE
            )
            coarse[at : at + tile, :] = jax.nn.gelu(now).astype(bf16)
        score = lax.dot_general(
            out_t[...], coarse[...], (((1,), (1,)), ((), ())), preferred_element_type=f32
        )
        result[n, 0:3, :] = (
            pixels[n, 0:3, :] + step_size * score + noise_gain * noise[n, 0:3, :]
        )
        return carry

    stream_halves = [halves.at[h] for h in range(depth // 128)]
    coarse[cells:, :] = jnp.zeros((coarse.shape[0] - cells, depth), bf16)
    lax.fori_loop(0, count, one_image, 0)
    for n in range(count):
        for y in range(SIDE):
            purified[y, :, n, :] = result[n, 0:3, y * WIDE : y * WIDE + SIDE]
    swap.wait()


def run_score(images, noise_field, stem, level_one, down, level_two, up, out_t, mlp_in):
    depth = stem.shape[1]
    vmem = pl.BlockSpec(memory_space=pltpu.VMEM)
    anywhere = pl.BlockSpec(memory_space=pl.ANY)
    return pl.pallas_call(
        score_kernel,
        out_shape=(
            jax.ShapeDtypeStruct(images.shape, f32),
            jax.ShapeDtypeStruct((mlp_in.shape[0], mlp_in.shape[1] // 2), bf16),
        ),
        in_specs=[vmem] * 3 + [anywhere] * 4 + [vmem, anywhere],
        out_specs=(vmem, anywhere),
        scratch_shapes=[
            pltpu.VMEM((images.shape[2], 8, WIDE * WIDE), f32),
            pltpu.VMEM((images.shape[2], 8, WIDE * WIDE), f32),
            pltpu.VMEM((images.shape[2], 8, WIDE * WIDE), f32),
            pltpu.VMEM((128, depth), f32),
            pltpu.VMEM(level_one.shape, bf16),
            pltpu.VMEM(down.shape, bf16),
            pltpu.VMEM(level_two.shape, bf16),
            pltpu.VMEM(up.shape, bf16),
            pltpu.VMEM(((SIDE + 2) * WIDE, 3 * depth), bf16),
            pltpu.VMEM(((SIDE + 2) * WIDE, 3 * depth), bf16),
            pltpu.VMEM(((HALF + 2) * HWIDE, 3 * depth), bf16),
            pltpu.VMEM(((HALF + 2) * HWIDE, 3 * depth), bf16),
            pltpu.VMEM((SIDE * WIDE, depth), f32),
            pltpu.VMEM((depth // 128, SIDE * WIDE, 128), f32),
            pltpu.VMEM((WIDE * WIDE, depth), bf16),
            pltpu.SemaphoreType.DMA((7,)),
            pltpu.SemaphoreType.DMA((2,)),
        ],
        compiler_params=pltpu.CompilerParams(
            collective_id=0, has_side_effects=True, vmem_limit_bytes=60 * MIB
        ),
        cost_estimate=pl.CostEstimate(
            flops=10_000_000_000, bytes_accessed=30_000_000, transcendentals=0
        ),
    )(images, noise_field, stem, level_one, down, level_two, up, out_t, mlp_in)


def mlp_kernel(
    rows,
    cols,
    chunk,
    patches,
    embed_weight,
    embed_bias,
    mlp_in,
    in_swapped,
    mlp_out,
    encoded,
    own_patches,
    row_patches,
    all_patches,
    embed_w,
    w_in,
    w_out,
    w_other,
    statistics,
    values,
    normed,
    partial_out,
    partial_in,
    hidden,
    total,
    pair_out,
    pair_in,
    last_out,
    last_in,
    load_sem,
    gather_send,
    gather_recv,
    spread_send,
    spread_recv,
    share_send,
    share_recv,
    rs_send,
    rs_recv,
    ag_send,
    ag_recv,
    swap_sem,
    pair_send,
    pair_recv,
    last_send,
    last_recv,
):
    row = lax.axis_index("row")
    col = lax.axis_index("col")
    z = col // 2
    core = col % 2
    depth = cols // 2
    last = depth - 1
    sibling = {"col": col + 1 - 2 * core}
    width = w_in.shape[2]
    height = w_out.shape[0]

    loads = [
        pltpu.make_async_copy(embed_weight, embed_w, load_sem.at[0]),
        pltpu.make_async_copy(
            mlp_in.at[:, pl.ds(pl.multiple_of(core * width, 128), width)],
            w_in.at[core],
            load_sem.at[1],
        ),
        pltpu.make_async_copy(in_swapped, w_in.at[1 - core], load_sem.at[2]),
        pltpu.make_async_copy(
            mlp_out.at[pl.ds(pl.multiple_of(core * height, 16), height), :],
            w_out,
            load_sem.at[3],
        ),
    ]
    for load in loads:
        load.start()
    own_patches[...] = patches[...]

    barrier = pltpu.get_barrier_semaphore()
    for step in range(1, cols):
        pl.semaphore_signal(
            barrier, inc=1, device_id={"col": (col + step) % cols}, device_id_type=MESH
        )
    for step in range(1, rows):
        pl.semaphore_signal(
            barrier, inc=1, device_id={"row": (row + step) % rows}, device_id_type=MESH
        )
    pl.semaphore_wait(barrier, cols - 1 + rows - 1)

    gathers = [
        remote(
            own_patches,
            row_patches.at[col],
            gather_send.at[step],
            gather_recv.at[step],
            {"col": (col + step) % cols},
        )
        for step in range(1, cols)
    ]
    for gather in gathers:
        gather.start()
    row_patches[col] = own_patches[...]
    for gather in gathers:
        gather.wait_recv()
    per_row = row_patches.shape[0] * row_patches.shape[1]
    all_patches[row] = row_patches[...].reshape(per_row, row_patches.shape[2]).astype(bf16)
    spreads = [
        remote(
            all_patches.at[row],
            all_patches.at[row],
            spread_send.at[step],
            spread_recv.at[step],
            {"row": (row + step) % rows},
        )
        for step in range(1, rows)
    ]
    for spread in spreads:
        spread.start()
    tokens = rows * per_row
    part_rows = per_row // 2
    pixels = embed_w.shape[0]
    features = embed_w.shape[1]
    span = features // cols
    loads[0].wait()

    def embed(tokens_in, at):
        at = pl.multiple_of(at, 128)
        return (
            (dot(tokens_in, embed_w[:, pl.ds(at, span)]) + embed_bias[0:1, pl.ds(at, span)])
            .astype(bf16)
            .astype(f32)
        )

    row_tokens = all_patches[row][:, 0:pixels]

    def add_statistics(step, sums):
        part = embed(row_tokens, step * span)
        return (
            sums[0] + jnp.sum(part, axis=1, keepdims=True),
            sums[1] + jnp.sum(part * part, axis=1, keepdims=True),
        )

    zeros = jnp.zeros((per_row, 1), f32)
    value_sums, square_sums = lax.fori_loop(0, cols, add_statistics, (zeros, zeros))
    mean = value_sums / features
    scale = lax.rsqrt(square_sums / features - mean * mean + ln_epsilon)
    lane = lax.broadcasted_iota(jnp.int32, (per_row, 128), 1)
    statistics[row] = jnp.where(lane < 64, mean, scale)
    shares = [
        remote(
            statistics.at[row],
            statistics.at[row],
            share_send.at[step],
            share_recv.at[step],
            {"row": (row + step) % rows},
        )
        for step in range(1, rows)
    ]
    for share in shares:
        share.start()
    for spread in spreads:
        spread.wait_recv()
    swap = remote(
        mlp_out.at[pl.ds(pl.multiple_of((1 - core) * height, 16), height), :],
        w_other,
        swap_sem.at[0],
        swap_sem.at[1],
        sibling,
    )
    swap.start()

    all_tokens = all_patches[...].reshape(tokens, all_patches.shape[2])[:, 0:pixels]
    for j in range(2):
        values[j] = embed(all_tokens, (2 * z + j) * span)
    for share in shares:
        share.wait_recv()
    for half in range(2):
        rows_in = pl.ds(half * part_rows, part_rows)
        known = statistics[:, rows_in, :].reshape(tokens // 2, 128)
        for j in range(2):
            part = values[j].reshape(rows, per_row, span)[
                :, half * part_rows : (half + 1) * part_rows
            ].reshape(tokens // 2, span)
            normed[j, half] = ((part - known[:, 0:1]) * known[:, 64:65]).astype(bf16)
            total[j, half] = jnp.zeros((tokens // 2, span), f32)
    loads[1].wait()
    loads[2].wait()

    chunks = partial_out.shape[1]
    per_half = chunks // 2
    place = (z, last - z)
    ahead = ({"col": col + 2}, {"col": col - 2})
    behind = ({"col": col - 2}, {"col": col + 2})

    def rs_copy(d, i):
        return remote(
            partial_out.at[d, i], partial_in.at[d, i], rs_send.at[d, i], rs_recv.at[d, i], ahead[d]
        )

    def ag_copy(d, i):
        return remote(
            hidden.at[d, i], hidden.at[d, i], ag_send.at[d, i], ag_recv.at[d, i], behind[d]
        )

    def pair_copy(half):
        return remote(
            pair_out.at[half],
            pair_in.at[half],
            pair_send.at[half],
            pair_recv.at[half],
            sibling,
        )

    def final_copies(half):
        return [
            remote(
                last_out.at[half, (row + step) % rows],
                last_in.at[half, step],
                last_send.at[half, step],
                last_recv.at[half, step],
                {"row": (row + step) % rows},
            )
            for step in range(1, rows)
        ]

    def pair_up(half):
        pair_out[half] = total[1, half].astype(bf16)
        pair_copy(half).start()

    def send_final(half):
        pair_copy(half).wait_recv()
        summed = total[0, half] + pair_in[half].astype(f32)
        last_out[half] = summed.astype(bf16).reshape(rows, part_rows, span)
        for final in final_copies(half):
            final.start()

    def finish(half):
        at = pl.ds(pl.multiple_of(row * per_row + half * part_rows, 16), part_rows)
        result = values[core, at, :] + last_out[half, row].astype(f32)
        for step, final in enumerate(final_copies(half)):
            final.wait_recv()
            result = result + last_in[half, step + 1].astype(f32)
        encoded[half * part_rows : (half + 1) * part_rows, :] = result.astype(bf16)

    first_done = per_half - 1 + LAG * (2 * last - jnp.minimum(place[0], place[1]))

    def slot(t, carry):
        @pl.when(t == LAG * last)
        def _():
            loads[3].wait()
            swap.wait_recv()

        for d in range(2):
            i = t - LAG * (2 * last - place[d])

            @pl.when((i >= 0) & (i < chunks) & (place[d] < last))
            def _():
                ag_copy(d, i).wait_recv()

                @pl.when(place[d] > 0)
                def _():
                    ag_copy(d, i).start()

        for d in range(2):
            i = t - LAG * place[d]

            @pl.when((i >= 0) & (i < chunks))
            def _():
                half = i // per_half
                at = pl.multiple_of((d * per_half + i % per_half) * chunk, chunk)
                mine = dot(normed[0, half], w_in[0, :, pl.ds(at, chunk)]) + dot(
                    normed[1, half], w_in[1, :, pl.ds(at, chunk)]
                )

                @pl.when(place[d] == 0)
                def _():
                    partial_out[d, i] = mine.astype(bf16)

                @pl.when(place[d] > 0)
                def _():
                    rs_copy(d, i).wait_recv()
                    whole = mine + partial_in[d, i].astype(f32)

                    @pl.when(place[d] < last)
                    def _():
                        partial_out[d, i] = whole.astype(bf16)

                    @pl.when(place[d] == last)
                    def _():
                        hidden[d, i] = jax.nn.gelu(whole).astype(bf16)

                @pl.when(place[d] < last)
                def _():
                    rs_copy(d, i).start()

                @pl.when(place[d] == last)
                def _():
                    ag_copy(d, i).start()

        for d in range(2):
            i = t - LAG * (2 * last - place[d])

            @pl.when((i >= 0) & (i < chunks))
            def _():
                half = i // per_half
                at = pl.multiple_of((d * per_half + i % per_half) * chunk, chunk)
                total[0, half] += dot(hidden[d, i], w_out[pl.ds(at, chunk), :])
                total[1, half] += dot(hidden[d, i], w_other[pl.ds(at, chunk), :])

        @pl.when(t == first_done)
        def _():
            pair_up(0)

        @pl.when(t == first_done + 2)
        def _():
            send_final(0)

        return carry

    lax.fori_loop(0, chunks + 2 * LAG * last, slot, 0)

    pair_up(1)
    finish(0)
    send_final(1)
    finish(1)

    finals = [final for half in range(2) for final in final_copies(half)]
    pairs = [pair_copy(half) for half in range(2)]
    for copy in gathers + spreads + shares + finals + pairs + [swap]:
        copy.wait_send()

    def drain(i, carry):
        for d in range(2):

            @pl.when(place[d] < last)
            def _():
                rs_copy(d, i).wait_send()

            @pl.when(place[d] > 0)
            def _():
                ag_copy(d, i).wait_send()

        return carry

    lax.fori_loop(0, chunks, drain, 0)


def run_mlp(
    rows, cols, patches, embed_weight, embed_bias, mlp_in, in_swapped, mlp_out
):
    per_device, pixels = patches.shape
    per_row = cols * per_device
    tokens = rows * per_row
    features = embed_weight.shape[1]
    span = features // cols
    width = in_swapped.shape[1]
    chunk = min(256, width // 2)
    chunks = 2 * (width // 2 // chunk)
    half = tokens // 2
    vmem = pl.BlockSpec(memory_space=pltpu.VMEM)
    anywhere = pl.BlockSpec(memory_space=pl.ANY)
    dma = pltpu.SemaphoreType.DMA
    return pl.pallas_call(
        functools.partial(mlp_kernel, rows, cols, chunk),
        out_shape=jax.ShapeDtypeStruct((per_row, span), bf16),
        in_specs=[vmem, anywhere, vmem, anywhere, anywhere, anywhere],
        out_specs=vmem,
        scratch_shapes=[
            pltpu.VMEM((per_device, pixels), f32),
            pltpu.VMEM((cols, per_device, pixels), f32),
            pltpu.VMEM((rows, per_row, pixels), bf16),
            pltpu.VMEM(embed_weight.shape, bf16),
            pltpu.VMEM((2,) + in_swapped.shape, bf16),
            pltpu.VMEM((width, span), bf16),
            pltpu.VMEM((width, span), bf16),
            pltpu.VMEM((rows, per_row, 128), f32),
            pltpu.VMEM((2, tokens, span), f32),
            pltpu.VMEM((2, 2, half, span), bf16),
            pltpu.VMEM((2, chunks, half, chunk), bf16),
            pltpu.VMEM((2, chunks, half, chunk), bf16),
            pltpu.VMEM((2, chunks, half, chunk), bf16),
            pltpu.VMEM((2, 2, half, span), f32),
            pltpu.VMEM((2, half, span), bf16),
            pltpu.VMEM((2, half, span), bf16),
            pltpu.VMEM((2, rows, per_row // 2, span), bf16),
            pltpu.VMEM((2, rows, per_row // 2, span), bf16),
            dma((4,)),
            dma((cols,)),
            dma((cols,)),
            dma((rows,)),
            dma((rows,)),
            dma((rows,)),
            dma((rows,)),
            dma((2, chunks)),
            dma((2, chunks)),
            dma((2, chunks)),
            dma((2, chunks)),
            dma((2,)),
            dma((2,)),
            dma((2,)),
            dma((2, rows)),
            dma((2, rows)),
        ],
        compiler_params=pltpu.CompilerParams(
            collective_id=1, has_side_effects=True, vmem_limit_bytes=56 * MIB
        ),
        cost_estimate=pl.CostEstimate(
            flops=10_000_000_000, bytes_accessed=30_000_000, transcendentals=0
        ),
    )(patches, embed_weight, embed_bias, mlp_in, in_swapped, mlp_out)


def on_device(
    images,
    noise_field,
    stem_weight,
    level_one,
    down_weight,
    level_two,
    up_weight,
    out_weight,
    embed_weight,
    embed_bias,
    mlp_in,
    mlp_out,
):
    rows = lax.axis_size("row")
    cols = lax.axis_size("col")
    lines, in_swapped = run_score(
        images.transpose(1, 3, 0, 2),
        noise_field.transpose(1, 3, 0, 2),
        stem_weight,
        level_one,
        down_weight,
        level_two,
        up_weight,
        out_weight.T,
        mlp_in,
    )
    count = images.shape[0]
    purified = lines.transpose(2, 0, 3, 1)
    grid = SIDE // PATCH
    patches = lines.astype(bf16).reshape(grid, PATCH, 3, count, grid, PATCH)
    patches = patches.transpose(3, 0, 4, 1, 5, 2).reshape(count * grid * grid, PATCH * PATCH * 3)
    pixels = patches.shape[1]
    patches = jnp.pad(patches.astype(f32), ((0, 0), (0, -pixels % 128)))
    encoded = run_mlp(
        rows,
        cols,
        patches,
        embed_weight,
        embed_bias[None, :],
        mlp_in,
        in_swapped,
        mlp_out,
    )
    return (purified, encoded)


def solution(mesh):
    placed = (
        P(("row", "col"), None, None, None),
        P(("row", "col"), None, None, None),
        P(),
        P(),
        P(),
        P(),
        P(),
        P(),
        P(),
        P(),
        P("col", "row"),
        P("row", "col"),
    )
    return jax.shard_map(
        on_device,
        mesh=mesh,
        in_specs=placed,
        out_specs=(P(("row", "col"), None, None, None), P("row", "col")),
        check_vma=False,
    )
```
